512 devices in a mesh: ctx: 32 (over z, core), exp: 16 (over y, x).
Axes of the slice: x: 4, y: 4, z: 16, core: 2. Of those that a mesh axis runs over, the one named last changes fastest.
Arguments:
- tokens: bfloat16 [16384, 4096], P('ctx', 'exp'), may hold values from -7 to 7
- expert_ids: int32 [16384, 8], P('ctx'), may hold values from 0 to 31, all different within a row; in each aligned block of 512 rows (0 to 511, 512 to 1023, ...) at most 160 rows name the same one
- gate_weights: float32 [16384, 8], P('ctx'), may hold values from 0.1 to 1
- query_weight: bfloat16 [32, 4096, 128], P('exp'), may hold values from -2.578125 to 2.578125
- key_weight: bfloat16 [4096, 128], P('exp'), may hold values from -0.09375 to 0.09375
- value_weight: bfloat16 [4096, 128], P('exp'), may hold values from -0.09375 to 0.09375
- output_weight: bfloat16 [32, 128, 4096], P('exp'), may hold values from -0.5 to 0.5
Outputs:
- mixed_rows: bfloat16 [16384, 4096], P('ctx', 'exp')
The draws below stay inside these ranges and needn't reach their ends.
Inputs may be any that keep to these rules, and one draw needn't show every extreme that they name: `expert_ids`: A token names 8 different head experts; among the tokens of one context shard (aligned blocks of 512 tokens) no head expert is named more than 160 times, and in every draw some head expert is named exactly 160 times in some block.
All inputs are finite; a program needn't handle non-finite values.
Results may differ from the reference program's by a relative error of at most 0.035.
Values may be sent and summed in bfloat16 or wider, within the bound.
A program may use at most 128 MiB of HBM per device.

```python
import math
import jax
import jax.numpy as jnp
import numpy as np
from jax import lax

D = 4096
HD = 128
TOP = 8
TOK_CTX = 512
E = 32
SEQ = 16384
CAP = 160


def shared_basis(key):
    key = jax.random.fold_in(key, 5)
    basis = jax.random.normal(key, (D, HD), jnp.float32)
    return jnp.clip(basis, -6.0, 6.0) / math.sqrt(D)


def draw_tokens(key, part):
    key = jax.random.fold_in(key, 11)
    first = jax.random.fold_in(key, 0)
    values = jnp.clip(jax.random.normal(first, (SEQ, D), jnp.float32), -6.0, 6.0)
    return values.astype(jnp.bfloat16)


def draw_key_weight(key, part):
    basis = shared_basis(key)
    return basis.astype(jnp.bfloat16)


def draw_query_weight(key, part):
    key = jax.random.fold_in(key, 17)
    first = jax.random.fold_in(key, 0)
    weights = jnp.clip(jax.random.normal(first, (E, D, HD), jnp.float32), -6.0, 6.0) * (2.5 / math.sqrt(D))
    return weights.astype(jnp.bfloat16)


def block_scale(rng, dims, shards, smallest, largest):
    def one(dim, blocks):
        draws = jax.random.uniform(jax.random.fold_in(jax.random.fold_in(rng, 6), dim), (blocks,), jnp.float32, smallest / len(shards), largest / len(shards))
        return jnp.repeat(jnp.exp(draws), dims[dim] // blocks).reshape((-1,) + (1,) * (len(dims) - dim - 1))

    factor_of = one(*shards[0])
    for cut in shards[1:]:
        factor_of = factor_of * one(*cut)
    return factor_of


def deal_out(key, own, number, rows, count, top, limit, skew):
    order = jax.random.permutation(key, count)
    heavy_load, ordinary = shares(count, rows * top, limit, skew, True), shares(count, rows * top, limit, skew, False)
    places = jnp.arange(count)

    def named(tallies, offset_by):
        used = int((tallies > 0).sum())
        fixed = max(1, used // 4)
        passed = fixed + (places - fixed + offset_by * (used - fixed)) % max(1, count - fixed)
        return jnp.zeros((count,), jnp.int32).at[order[jnp.where(places < fixed, places, passed)]].set(jnp.asarray(tallies, jnp.int32))

    tallies = jnp.where(number % 4 == 0, named(heavy_load, number // 4), named(ordinary, number - number // 4 - 1))
    mixed = jax.random.permutation(jax.random.fold_in(own, 3), count)
    donor, taker = mixed[0:count // 2 * 2:2], mixed[1:count // 2 * 2:2]
    margin = jnp.minimum(tallies[donor] - 1, limit - tallies[taker]) // 2
    margin = jnp.where((donor == order[0]) | (taker == order[0]) | (tallies[taker] == 0), 0, jnp.maximum(margin, 0))
    passed = jax.random.randint(jax.random.fold_in(own, 4), (count // 2,), 0, 1 << 20) % (margin + 1)
    tallies = tallies.at[donor].add(-passed).at[taker].add(passed)
    items = jnp.searchsorted(jnp.cumsum(tallies), jnp.arange(rows * top), side="right").astype(jnp.int32)
    grid = items.reshape(top, rows).T
    grid = grid[jax.random.permutation(jax.random.fold_in(own, 1), rows)]
    offset_by = jax.random.randint(jax.random.fold_in(own, 2), (rows, 1), 0, top)
    return jnp.take_along_axis(grid, (jnp.arange(top)[None, :] + offset_by) % top, axis=1)


def shares(count, total, most, skew, full):
    portions = [(1 << 20) // math.isqrt(standing ** skew) + 1 for standing in range(1, count + 1)]
    largest = most if full else min(most, max(-(-total // count), total * portions[0] // sum(portions)))
    least = 1 if total - largest >= count - 1 else 0
    holding, surplus = [largest] + [least] * (count - 1), total - largest - least * (count - 1)
    while surplus > 0:
        movable = [i for i in range(1, count) if holding[i] < largest] or [i for i in range(1, count) if holding[i] < most]
        pool, left = sum([portions[i] for i in movable]), surplus
        for i in movable:
            addition = min(most - holding[i], max(1, left * portions[i] // pool), surplus)
            holding[i] = holding[i] + addition
            surplus = surplus - addition
    return np.array(holding)


def scatter_about(stream_key, shape, spread, reach, cuts=(), kind=jnp.bfloat16):
    result = jax.random.normal(stream_key, shape, jnp.float32) * spread
    if len(cuts) > 0:
        result = block_scale(stream_key, shape, cuts, -0.22, 0.18) * result
    return jnp.clip(result, min=-reach, max=reach).astype(kind)


def setup_inputs(seed: int = 0) -> dict:
    splits = jax.random.split(jax.random.key(seed), 8)
    tokens = draw_tokens(jax.random.fold_in(splits[7], 71), 0)
    expert_ids_keys = jax.random.split(jax.random.fold_in(splits[1], 1), SEQ // TOK_CTX)
    expert_ids_turns = jax.random.permutation(jax.random.fold_in(splits[1], 3), SEQ // TOK_CTX)
    expert_ids = jax.vmap(lambda own, number: deal_out(jax.random.fold_in(splits[1], 2), own, number, TOK_CTX, E, TOP, CAP, 2))(expert_ids_keys, expert_ids_turns).reshape((SEQ, TOP))
    gate_weights = jnp.clip(0.1 + 0.9 * jax.random.uniform(splits[2], (SEQ, TOP), jnp.float32) ** block_scale(splits[2], (SEQ, TOP), ((0, 32),), -0.2, 0.2), 0.1, 1.0)
    query_weight = draw_query_weight(jax.random.fold_in(splits[7], 71), 0)
    key_weight = draw_key_weight(jax.random.fold_in(splits[7], 71), 0)
    value_weight = scatter_about(splits[5], (D, HD), D ** -0.5, 0.09375, ((0, 16),))
    output_weight = scatter_about(splits[6], (E, HD, D), HD ** -0.5, 0.5, ((0, 16),))
    return {"tokens": tokens, "expert_ids": expert_ids, "gate_weights": gate_weights, "query_weight": query_weight, "key_weight": key_weight, "value_weight": value_weight, "output_weight": output_weight}


def route_slots(expert_ids):
    grouped = expert_ids.reshape(SEQ // TOK_CTX, TOK_CTX * TOP)
    one_hot = (grouped[:, :, None] == jnp.arange(E, dtype=jnp.int32)[None, None, :]).astype(jnp.int32)
    earlier = jnp.cumsum(one_hot, axis=1) - one_hot
    return lax.optimization_barrier(jnp.sum(earlier * one_hot, axis=2)).reshape(SEQ, TOP).astype(jnp.int32)

def reference(tokens, expert_ids, gate_weights, query_weight, key_weight, value_weight, output_weight):
    key_rows = jnp.dot(tokens, key_weight, preferred_element_type=jnp.float32).astype(jnp.bfloat16)
    value_rows = jnp.dot(tokens, value_weight, preferred_element_type=jnp.float32).astype(jnp.bfloat16)
    slot_index = route_slots(expert_ids)
    token_index = jnp.arange(SEQ, dtype=jnp.int32)
    column = ((token_index // TOK_CTX)[:, None] * CAP + slot_index).astype(jnp.int32)
    width_slots = SEQ // TOK_CTX * CAP
    token_table = jnp.zeros((E, width_slots), jnp.int32).at[expert_ids, column].set(jnp.broadcast_to(token_index[:, None], (SEQ, TOP)))
    route_table = jnp.zeros((E, width_slots), jnp.int32).at[expert_ids, column].set(jnp.broadcast_to(jnp.arange(TOP, dtype=jnp.int32)[None, :], (SEQ, TOP)))
    gate_table = jnp.zeros((E, width_slots), jnp.float32).at[expert_ids, column].set(gate_weights)

    def project_queries(inputs):
        rows_index, weight = inputs
        return jnp.dot(tokens[rows_index], weight, preferred_element_type=jnp.float32).astype(jnp.bfloat16)
    query_table = lax.map(project_queries, (token_table, query_weight))
    pair_queries = query_table[expert_ids, column]
    score_scale = 1.0 / math.sqrt(HD)
    head_blocks = []
    for segment in range(SEQ // TOK_CTX):
        lower = segment * TOK_CTX
        upper = lower + TOK_CTX
        block_queries = pair_queries[lower:upper].reshape(TOK_CTX * TOP, HD)
        scores = jnp.dot(block_queries, key_rows[:upper].T, preferred_element_type=jnp.float32) * score_scale
        positions = lower + jnp.arange(TOK_CTX * TOP, dtype=jnp.int32) // TOP
        visible = jnp.arange(upper, dtype=jnp.int32)[None, :] <= positions[:, None]
        masked = jnp.where(visible, scores, -1e+30)
        row_max = lax.optimization_barrier(jnp.max(masked, axis=1, keepdims=True))
        weights = jnp.where(visible, jnp.exp(masked - row_max), 0.0)
        weight_sum = lax.optimization_barrier(jnp.sum(weights, axis=1, keepdims=True))
        numerator = jnp.dot(weights.astype(jnp.bfloat16), value_rows[:upper], preferred_element_type=jnp.float32)
        head_blocks.append((numerator / weight_sum).astype(jnp.bfloat16))
    head_rows = jnp.concatenate(head_blocks, axis=0).reshape(SEQ, TOP, HD)

    def add_expert(running, inputs):
        rows_index, route_index, gate_row, weight = inputs
        produced = jnp.dot(head_rows[rows_index, route_index], weight, preferred_element_type=jnp.float32).astype(jnp.bfloat16)
        return (running.at[rows_index].add(gate_row[:, None] * produced.astype(jnp.float32)), None)
    mixed_rows, ignored = lax.scan(add_expert, jnp.zeros((SEQ, D), jnp.float32), (token_table, route_table, gate_table, output_weight))
    return mixed_rows.astype(jnp.bfloat16)
```

```python
import functools
import math

import jax
import jax.numpy as jnp
from jax import lax
from jax.experimental import pallas as pl
from jax.experimental.pallas import tpu as pltpu
from jax.sharding import PartitionSpec as P

MESH = pl.DeviceIdType.MESH
RING = 4
PEERS = RING * RING
LANES = 256
LOWEST = -1e30


def nt_dot(a, b):
    return lax.dot_general(a, b, (((1,), (1,)), ((), ())), preferred_element_type=jnp.float32)


def tn_dot(a, b):
    return lax.dot_general(a, b, (((0,), (0,)), ((), ())), preferred_element_type=jnp.float32)


def dot(a, b):
    return jnp.dot(a, b, preferred_element_type=jnp.float32)


def drain(ref, sem):
    pltpu.make_async_copy(ref, ref, sem).wait()


class PlaneGather:
    def __init__(self, buf, rows, send_sem, recv_sem, place):
        self.buf, self.rows = buf, rows
        self.send_sem, self.recv_sem, self.place = send_sem, recv_sem, place
        self.started = []

    def slot(self, half, first, second):
        return second * RING + first if half == 0 else first * RING + second

    def message(self, half, phase, other, where):
        rows = self.rows // 2
        index = {3: 0, 1: 1, "2a": 2, "2b": 3}[where]
        number = half * 20 + (index if phase == 0 else 4 + other * 4 + index)
        begin = half * rows
        if where in ("2a", "2b"):
            rows = rows // 2
            if where == "2b":
                begin += rows
        step = 1 if where in (3, "2a") else 3
        source = {3: 0, 1: 0, "2a": 3, "2b": 1}[where]
        target = int(str(where)[0])
        if phase == 0:
            src, dst = self.slot(half, source, 0), self.slot(half, target, 0)
        else:
            src, dst = self.slot(half, other, source), self.slot(half, other, target)
        along_x = (half == 0) == (phase == 0)
        device = self.place(0, step) if along_x else self.place(step, 0)
        return pltpu.make_async_remote_copy(
            src_ref=self.buf.at[src, pl.ds(begin, rows)],
            dst_ref=self.buf.at[dst, pl.ds(begin, rows)],
            send_sem=self.send_sem.at[number],
            recv_sem=self.recv_sem.at[number],
            device_id=device,
            device_id_type=MESH,
        )

    def start(self, *key):
        copy = self.message(*key)
        copy.start()
        self.started.append(copy)

    def wait(self, *key):
        self.message(*key).wait_recv()

    def finish(self):
        for copy in self.started:
            copy.wait_send()

    def run(self, arrived, beside=lambda stage: None):
        for half in range(2):
            self.start(half, 0, 0, 3)
            self.start(half, 0, 0, 1)
        for half in range(2):
            self.start(half, 1, 0, 3)
            self.start(half, 1, 0, 1)
        beside(0)
        arrived(0, 0)
        arrived(1, 0)
        for half in range(2):
            for where, onward in ((3, "2a"), (1, "2b")):
                self.wait(half, 0, 0, where)
                self.start(half, 0, 0, onward)
                self.start(half, 1, where, 3)
                self.start(half, 1, where, 1)
        for half in range(2):
            for where in (3, 1):
                arrived(half, self.slot(half, where, 0))
        beside(1)
        for half in range(2):
            for where, onward in ((3, "2a"), (1, "2b")):
                self.wait(half, 1, 0, where)
                self.start(half, 1, 0, onward)
        for half in range(2):
            self.wait(half, 0, 0, "2a")
            self.wait(half, 0, 0, "2b")
            self.start(half, 1, 2, 3)
            self.start(half, 1, 2, 1)
        for half in range(2):
            for where in (3, 1):
                arrived(half, self.slot(half, 0, where))
            arrived(half, self.slot(half, 2, 0))
        beside(2)
        for other in (3, 1):
            for half in range(2):
                for where, onward in ((3, "2a"), (1, "2b")):
                    self.wait(half, 1, other, where)
                    self.start(half, 1, other, onward)
                    arrived(half, self.slot(half, other, where))
        beside(3)
        for half in range(2):
            self.wait(half, 1, 0, "2a")
            self.wait(half, 1, 0, "2b")
            arrived(half, self.slot(half, 0, 2))
        for half in range(2):
            for where, onward in ((3, "2a"), (1, "2b")):
                self.wait(half, 1, 2, where)
                self.start(half, 1, 2, onward)
                arrived(half, self.slot(half, 2, where))
        beside(4)
        for other in (3, 1, 2):
            for half in range(2):
                self.wait(half, 1, other, "2a")
                self.wait(half, 1, other, "2b")
                arrived(half, self.slot(half, other, 2))
        beside(5)


def layer(
    capacity,
    tokens,
    expert_ids,
    gates,
    query_weight,
    key_weight,
    value_weight,
    output_weight,
    out,
    tok,
    qw,
    kv_part,
    kv_in,
    kv,
    q_sum,
    q_all,
    slot_of,
    gate_of,
    spread,
    where_row,
    wout,
    top_score,
    num,
    part_out,
    part_lse,
    heads,
    produced,
    total,
    tok_send,
    tok_recv,
    head_send,
    head_recv,
    peer_send,
    peer_recv,
    local,
):
    ctx, exp = lax.axis_index("ctx"), lax.axis_index("exp")
    y, x = exp // RING, exp % RING
    z, core = ctx // 2, ctx % 2
    depth = kv.shape[0]
    t, f = tokens.shape
    routes = expert_ids.shape[1]
    mine = query_weight.shape[0]
    hd = query_weight.shape[2]
    share = t // PEERS
    owned = mine * capacity

    def place(dy, dx):
        return (ctx, ((y + dy) % RING) * RING + (x + dx) % RING)

    sibling = (ctx + 1 - 2 * core, exp)

    def send(src, dst, send_sem, recv_sem, device):
        return pltpu.make_async_remote_copy(
            src_ref=src, dst_ref=dst, send_sem=send_sem, recv_sem=recv_sem, device_id=device, device_id_type=MESH
        )

    barrier = pltpu.get_barrier_semaphore()

    @pl.loop(1, PEERS)
    def _(i):
        pl.semaphore_signal(barrier, inc=1, device_id=(ctx, (exp + i) % PEERS), device_id_type=MESH)

    @pl.loop(1, depth)
    def _(i):
        pl.semaphore_signal(barrier, inc=1, device_id=(((z + i) % depth) * 2 + core, exp), device_id_type=MESH)

    pl.semaphore_signal(barrier, inc=1, device_id=sibling, device_id_type=MESH)

    load_qw = pltpu.make_async_copy(query_weight, qw, local.at[0])
    load_qw.start()
    own_width = pl.ds(pl.multiple_of(exp * f, f), f)
    load_wout = pltpu.make_async_copy(output_weight.at[core, :, own_width], wout.at[0, core], local.at[1])
    load_wout.start()

    tok[0] = tokens[...]
    kv_part[:, :hd] = dot(tokens[...], key_weight[...]).astype(jnp.bfloat16)
    kv_part[:, hd:] = dot(tokens[...], value_weight[...]).astype(jnp.bfloat16)

    column = lax.broadcasted_iota(jnp.int32, (1, 128), 1)
    at = column // mine
    expert = ((((y + at // RING) % RING) * RING) + (x + at % RING) % RING) * mine + column % mine
    routed = jnp.zeros((t, 128), jnp.float32)
    gate_sum = jnp.zeros((t, 128), jnp.float32)
    for r in range(routes):
        hit = expert_ids[:, r : r + 1] == expert
        routed = jnp.where(hit, 1.0, routed)
        gate_sum = jnp.where(hit, gates[:, r : r + 1], gate_sum)
    gate_of[...] = gate_sum
    earlier = jnp.where(
        lax.broadcasted_iota(jnp.int32, (t, t), 1) < lax.broadcasted_iota(jnp.int32, (t, t), 0), 1.0, 0.0
    ).astype(jnp.bfloat16)
    slot_of[...] = jnp.where(routed > 0.5, dot(earlier, routed.astype(jnp.bfloat16)), -1.0)

    pl.semaphore_wait(barrier, PEERS - 1 + depth - 1 + 1)

    @pl.loop(1, PEERS)
    def _(i):
        j = (exp + i) % PEERS
        send(
            kv_part.at[pl.ds(pl.multiple_of(j * share, share), share)],
            kv_in.at[i],
            peer_send.at[0],
            peer_recv.at[0],
            (ctx, j),
        ).start()

    gather = PlaneGather(tok, t, tok_send, tok_recv, place)
    q_sum[...] = jnp.zeros_like(q_sum)

    def add_queries(half, slot):
        rows = pl.ds(half * (t // 2), t // 2)
        owner = ((y + slot // RING) % RING) * RING + (x + slot % RING) % RING
        features = pl.ds(pl.multiple_of(owner * f, f), f)
        piece = tok[slot, rows]
        for a in range(mine):
            q_sum[a, rows] += dot(piece, qw[a, features])

    x1, x2, x3 = (x + 1) % RING, (x + 2) % RING, (x + 3) % RING
    half_z = depth // 2
    lower, upper = pl.ds(0, half_z), pl.ds(half_z, half_z)
    to_right = send(kv.at[:, core, x], kv.at[:, core, x], peer_send.at[2], peer_recv.at[2], place(0, 1))
    to_left = send(kv.at[:, core, x], kv.at[:, core, x], peer_send.at[3], peer_recv.at[3], place(0, 3))
    on_right = send(kv.at[lower, core, x3], kv.at[lower, core, x3], peer_send.at[4], peer_recv.at[4], place(0, 1))
    on_left = send(kv.at[upper, core, x1], kv.at[upper, core, x1], peer_send.at[5], peer_recv.at[5], place(0, 3))

    def got(piece, number, device):
        return send(piece, piece, peer_send.at[number], peer_recv.at[number], device)

    from_left = got(kv.at[:, core, x3], 2, place(0, 1))
    from_right = got(kv.at[:, core, x1], 3, place(0, 3))
    far_lower = got(kv.at[lower, core, x2], 4, place(0, 1))
    far_upper = got(kv.at[upper, core, x2], 5, place(0, 3))
    across = [
        send(kv.at[:, core, xx], kv.at[:, core, xx], peer_send.at[6 + n], peer_recv.at[6 + n], sibling)
        for n, xx in enumerate((x, x3, x1, x2))
    ]
    other_core = 1 - core
    across_in = [
        got(kv.at[:, other_core, xx], 6 + n, sibling) for n, xx in enumerate((x, x3, x1, x2))
    ]

    def one_hot(n, values):
        lane = lax.broadcasted_iota(jnp.int32, (t, 128), 1)
        pick = lane == n
        slot = jnp.sum(jnp.where(pick, slot_of[...], 0.0), axis=1, keepdims=True)
        if values is None:
            value = jnp.ones((t, 1), jnp.float32)
        else:
            value = jnp.sum(jnp.where(pick, values[...], 0.0), axis=1, keepdims=True)
        lanes = lax.broadcasted_iota(jnp.int32, (t, LANES), 1).astype(jnp.float32)
        return jnp.where(slot == lanes, value, 0.0).astype(jnp.bfloat16)

    def beside(stage):
        if stage == 0:
            drain(kv_in.at[pl.ds(1, PEERS - 1)], peer_recv.at[0])
            summed = kv_part[pl.ds(pl.multiple_of(exp * share, share), share)].astype(jnp.float32)
            for i in range(1, PEERS):
                summed += kv_in[i].astype(jnp.float32)
            kv[z, core, x] = summed.astype(jnp.bfloat16)

            @pl.loop(1, depth)
            def _(i):
                zz = (z + i) % depth
                send(
                    kv.at[z, core, x], kv.at[z, core, x], peer_send.at[1], peer_recv.at[1], (zz * 2 + core, exp)
                ).start()

            load_qw.wait()
        elif stage == 1:

            @pl.loop(0, PEERS * mine)
            def _(n):
                spread[n] = one_hot(n, gate_of)

        elif stage == 2:
            position = lax.broadcasted_iota(jnp.int32, (t, 128), 0)
            high = (position // 16).astype(jnp.float32).astype(jnp.bfloat16)
            low = (position % 16).astype(jnp.float32).astype(jnp.bfloat16)
            place_of = jnp.concatenate([high, low], axis=1)

            @pl.loop(0, RING * mine)
            def _(n):
                at = tn_dot(one_hot((n // mine) * (RING * mine) + n % mine, None), place_of)
                where_row[n] = 16.0 * at[:capacity, :128] + at[:capacity, 128:]

        elif stage == 3:
            drain(kv.at[pl.ds(1, depth - 1), core, x], peer_recv.at[1])
            to_right.start()
            to_left.start()
            across[0].start()
        elif stage == 4:
            from_left.wait_recv()
            on_right.start()
            across[1].start()
            from_right.wait_recv()
            on_left.start()
            across[2].start()

    gather.run(add_queries, beside)

    for a in range(mine):
        rows = q_sum[a].astype(jnp.bfloat16)
        q_all[0, pl.ds(a * capacity, capacity)] = tn_dot(one_hot(a, None), rows)[:capacity].astype(jnp.bfloat16)
    q_moves = [
        send(q_all.at[0], q_all.at[RING - dy], peer_send.at[10 + dy], peer_recv.at[10 + dy], place(dy, 0))
        for dy in range(1, RING)
    ]
    for move in q_moves:
        move.start()

    far_lower.wait_recv()
    far_upper.wait_recv()
    across[3].start()

    @pl.loop(1, PEERS)
    def _(i):
        dy, dx = i // RING, i % RING
        j = ((y + dy) % RING) * RING + (x + dx) % RING
        back = ((RING - dy) % RING) * RING + (RING - dx) % RING
        send(
            output_weight.at[core, :, pl.ds(pl.multiple_of(j * f, f), f)],
            wout.at[back, core],
            peer_send.at[16],
            peer_recv.at[16],
            (ctx, j),
        ).start()

    for copy in across_in:
        copy.wait_recv()

    factor = math.log2(math.e) / math.sqrt(hd)
    groups = ctx // 4
    block = 4 * RING * share

    def attend(dy):
        top_score[...] = jnp.full_like(top_score, LOWEST)
        num[...] = jnp.zeros_like(num)

        def step(g, masked):
            keys = kv[pl.ds(2 * g, 2)].reshape(block, 2 * hd)
            values = jnp.concatenate([keys[:, hd:], jnp.ones((block, hd), jnp.bfloat16)], axis=1)
            keys = keys[:, :hd]
            for a in range(mine):
                rows = pl.ds(a * capacity, capacity)
                scores = nt_dot(q_all[dy, rows], keys)
                if masked:
                    index = lax.broadcasted_iota(jnp.int32, (1, block), 1)
                    span = RING * share
                    at = (4 * g + index // span - ctx) * t + y * span + index % span
                    scores = jnp.where(
                        at.astype(jnp.float32) <= where_row[dy * mine + a][:, 0:1], scores, LOWEST
                    )
                before = top_score[rows, 0:1]
                now = jnp.maximum(before, jnp.max(scores, axis=1, keepdims=True))
                weights = jnp.exp2((scores - now) * factor).astype(jnp.bfloat16)
                num[rows] = num[rows] * jnp.exp2((before - now) * factor) + dot(weights, values)
                top_score[rows] = jnp.broadcast_to(now, (capacity, 128))

        @pl.loop(0, groups)
        def _(g):
            step(g, False)

        step(groups, True)
        for a in range(mine):
            rows = pl.ds(a * capacity, capacity)
            norm = num[rows, hd:]
            part_out[dy, rows] = (num[rows, :hd] / norm).astype(jnp.bfloat16)
            lse = top_score[rows, 0:1] * factor + jnp.log2(norm[:, 0:1])
            part_lse[dy, pl.ds(a * 8, 8)] = to_row(lse)

    def diagonal():
        return lax.broadcasted_iota(jnp.int32, (capacity, LANES), 0) == lax.broadcasted_iota(
            jnp.int32, (capacity, LANES), 1
        )

    def to_row(values):
        row = jnp.sum(jnp.where(diagonal(), values, 0.0), axis=0, keepdims=True)
        return jnp.broadcast_to(row, (8, LANES))

    def to_column(row):
        return jnp.sum(jnp.where(diagonal(), row, 0.0), axis=1, keepdims=True)

    moves = []
    for dy in (2, 1, 3, 0):
        if dy:
            q_moves[RING - dy - 1].wait_recv()
        attend(dy)
        if dy:
            moves.append(
                send(part_out.at[dy], part_out.at[8 - dy], peer_send.at[17 + dy], peer_recv.at[17 + dy], place(dy, 0))
            )
            moves.append(
                send(part_lse.at[dy], part_lse.at[8 - dy], peer_send.at[21 + dy], peer_recv.at[21 + dy], place(dy, 0))
            )
            moves[-2].start()
            moves[-1].start()

    load_wout.wait()
    drain(wout.at[pl.ds(1, PEERS - 1), core], peer_recv.at[16])
    weights_across = send(wout.at[:, core], wout.at[:, core], peer_send.at[17], peer_recv.at[17], sibling)
    weights_across.start()
    produced[...] = jnp.zeros_like(produced)
    total[...] = jnp.zeros_like(total)

    for move in moves:
        move.wait_recv()
    for a in range(mine):
        rows = pl.ds(a * capacity, capacity)
        slots = (0, 5, 6, 7)
        lses = [to_column(part_lse[s, pl.ds(a * 8, 1)]) for s in slots]
        top = functools.reduce(jnp.maximum, lses)
        shares = [jnp.exp2(lse - top) for lse in lses]
        norm = functools.reduce(jnp.add, shares)
        rows_sum = functools.reduce(
            jnp.add, [w * part_out[s, rows].astype(jnp.float32) for w, s in zip(shares, slots)]
        )
        heads[0, rows] = (rows_sum / norm).astype(jnp.bfloat16)

    got(wout.at[:, other_core], 17, sibling).wait_recv()

    def add_output(half, slot):
        n = slot * mine + half
        made = dot(heads[slot, pl.ds(half * capacity, capacity)], wout[slot, half])
        produced[half, pl.ds(0, capacity)] = made.astype(jnp.bfloat16)
        total[...] += dot(spread[n], produced[half])

    head_gather = PlaneGather(heads, owned, head_send, head_recv, place)
    head_gather.run(add_output)
    out[...] = total[...].astype(jnp.bfloat16)

    gather.finish()
    head_gather.finish()
    drain(kv_in.at[pl.ds(1, PEERS - 1)], peer_send.at[0])
    drain(kv.at[pl.ds(1, depth - 1), core, x], peer_send.at[1])
    drain(wout.at[pl.ds(1, PEERS - 1), core], peer_send.at[16])
    for copy in (to_right, to_left, on_right, on_left, weights_across, *across, *q_moves, *moves):
        copy.wait_send()


def per_device(depth, tokens, expert_ids, gates, query_weight, key_weight, value_weight, output_weight):
    t, f = tokens.shape
    routes = expert_ids.shape[1]
    mine, model, hd = query_weight.shape
    experts = mine * PEERS
    capacity = min(t, max(2, 5 * t * routes // (4 * experts)))
    owned = mine * capacity
    share = t // PEERS
    bf16, f32 = jnp.bfloat16, jnp.float32
    vmem, anywhere = pl.BlockSpec(memory_space=pltpu.VMEM), pl.BlockSpec(memory_space=pl.ANY)
    return pl.pallas_call(
        functools.partial(layer, capacity),
        out_shape=jax.ShapeDtypeStruct((t, f), bf16),
        in_specs=[vmem, vmem, vmem, anywhere, vmem, vmem, anywhere],
        out_specs=vmem,
        scratch_shapes=[
            pltpu.VMEM((PEERS, t, f), bf16),
            pltpu.VMEM((mine, model, hd), bf16),
            pltpu.VMEM((t, 2 * hd), bf16),
            pltpu.VMEM((PEERS, share, 2 * hd), bf16),
            pltpu.VMEM((depth, 2, RING, share, 2 * hd), bf16),
            pltpu.VMEM((mine, t, hd), f32),
            pltpu.VMEM((RING, owned, hd), bf16),
            pltpu.VMEM((t, 128), f32),
            pltpu.VMEM((t, 128), f32),
            pltpu.VMEM((experts, t, LANES), bf16),
            pltpu.VMEM((RING * mine, capacity, 128), f32),
            pltpu.VMEM((PEERS, mine, hd, f), bf16),
            pltpu.VMEM((owned, 128), f32),
            pltpu.VMEM((owned, 2 * hd), f32),
            pltpu.VMEM((2 * RING, owned, hd), bf16),
            pltpu.VMEM((2 * RING, 8 * mine, LANES), f32),
            pltpu.VMEM((PEERS, owned, hd), bf16),
            pltpu.VMEM((mine, LANES, f), bf16),
            pltpu.VMEM((t, f), f32),
            pltpu.SemaphoreType.DMA((40,)),
            pltpu.SemaphoreType.DMA((40,)),
            pltpu.SemaphoreType.DMA((40,)),
            pltpu.SemaphoreType.DMA((40,)),
            pltpu.SemaphoreType.DMA((25,)),
            pltpu.SemaphoreType.DMA((25,)),
            pltpu.SemaphoreType.DMA((2,)),
        ],
        compiler_params=pltpu.CompilerParams(
            collective_id=0, has_side_effects=True, vmem_limit_bytes=56 * 1024 * 1024
        ),
    )(tokens, expert_ids, gates, query_weight, key_weight, value_weight, output_weight)


def solution(mesh):
    in_specs = (
        P("ctx", "exp"),
        P("ctx", None),
        P("ctx", None),
        P("exp", None, None),
        P("exp", None),
        P("exp", None),
        P("exp", None, None),
    )
    out_specs = P("ctx", "exp")
    return jax.shard_map(
        functools.partial(per_device, mesh.shape["ctx"] // 2),
        mesh=mesh,
        in_specs=in_specs,
        out_specs=out_specs,
        check_vma=False,
    )
```

```python
import functools
import math

import jax
import jax.numpy as jnp
from jax import lax
from jax.experimental import pallas as pl
from jax.experimental.pallas import tpu as pltpu
from jax.sharding import PartitionSpec as P

MESH = pl.DeviceIdType.MESH
RING = 4
PEERS = RING * RING
LANES = 256
LOWEST = -1e30


def nt_dot(a, b):
    return lax.dot_general(a, b, (((1,), (1,)), ((), ())), preferred_element_type=jnp.float32)


def tn_dot(a, b):
    return lax.dot_general(a, b, (((0,), (0,)), ((), ())), preferred_element_type=jnp.float32)


def dot(a, b):
    return jnp.dot(a, b, preferred_element_type=jnp.float32)


def drain(ref, sem):
    pltpu.make_async_copy(ref, ref, sem).wait()


class PlaneGather:
    STEPS = {3: 1, 1: 3, 2: 2}

    def __init__(self, buf, rows, send_sem, recv_sem, place):
        self.buf, self.rows = buf, rows // 2
        self.send_sem, self.recv_sem, self.place = send_sem, recv_sem, place
        self.started = []

    @staticmethod
    def slot(half, first, second):
        return second * RING + first if half == 0 else first * RING + second

    @staticmethod
    def order():
        slot = PlaneGather.slot
        pieces = [(half, slot(half, first, 0)) for first in (0, 3, 1, 2) for half in range(2)]
        pieces += [
            (half, slot(half, first, second)) for first in (0, 3, 1, 2) for second in (3, 1, 2) for half in range(2)
        ]
        return pieces

    def message(self, half, phase, other, where):
        number = half * PEERS + (where * RING if phase == 0 else other * RING + where)
        rows = pl.ds(half * self.rows, self.rows)
        if phase == 0:
            src, dst = self.slot(half, 0, 0), self.slot(half, where, 0)
        else:
            src, dst = self.slot(half, other, 0), self.slot(half, other, where)
        step = self.STEPS[where]
        along_x = (half == 0) == (phase == 0)
        return pltpu.make_async_remote_copy(
            src_ref=self.buf.at[src, rows],
            dst_ref=self.buf.at[dst, rows],
            send_sem=self.send_sem.at[number],
            recv_sem=self.recv_sem.at[number],
            device_id=self.place(0, step) if along_x else self.place(step, 0),
            device_id_type=MESH,
        )

    def start(self, *key):
        copy = self.message(*key)
        copy.start()
        self.started.append(copy)

    def wait(self, *key):
        self.message(*key).wait_recv()

    def finish(self):
        for copy in self.started:
            copy.wait_send()

    def run(self, arrived, beside):
        for where in (3, 1, 2):
            for half in range(2):
                self.start(half, 0, 0, where)
        for where in (3, 1, 2):
            for half in range(2):
                self.start(half, 1, 0, where)
        beside(0)
        for half in range(2):
            arrived(half, 0)
        for first in (3, 1, 2):
            for half in range(2):
                self.wait(half, 0, 0, first)
                for where in (3, 1, 2):
                    self.start(half, 1, first, where)
        for first in (3, 1, 2):
            for half in range(2):
                arrived(half, self.slot(half, first, 0))
        for first in (0, 3, 1, 2):
            for where in (3, 1, 2):
                for half in range(2):
                    self.wait(half, 1, first, where)
                    arrived(half, self.slot(half, first, where))
            beside({0: 1, 3: 2, 1: 3, 2: 4}[first])


def layer(
    capacity,
    depth,
    tokens,
    expert_ids,
    gates,
    query_weight,
    key_weight,
    value_weight,
    output_weight,
    out,
    tok,
    qw,
    kv_part,
    kv_in,
    kv,
    q_dense,
    q_part,
    q_all,
    slot_of,
    gate_of,
    slot_row,
    spread,
    pick,
    where_row,
    wout,
    top_score,
    num,
    part_out,
    part_lse,
    heads,
    produced,
    total,
    head_send,
    head_recv,
    send_sem,
    recv_sem,
    local,
):
    ctx, exp = lax.axis_index("ctx"), lax.axis_index("exp")
    y, x = exp // RING, exp % RING
    z, core = ctx // 2, ctx % 2
    m, r = z // RING, z % RING
    other_core = 1 - core
    t, f = tokens.shape
    routes = expert_ids.shape[0]
    mine = query_weight.shape[0]
    hd = query_weight.shape[2]
    share = t // PEERS
    wide = RING * f

    def place(dy, dx):
        return (ctx, ((y + dy) % RING) * RING + (x + dx) % RING)

    def deep(dz):
        return (((z + dz) % depth) * 2 + core, exp)

    sibling = (ctx + 1 - 2 * core, exp)
    used = []

    def send(src, dst, device, number=None):
        if number is None:
            number = len(used)
            used.append(number)
        return pltpu.make_async_remote_copy(
            src_ref=src,
            dst_ref=dst,
            send_sem=send_sem.at[number],
            recv_sem=recv_sem.at[number],
            device_id=device,
            device_id_type=MESH,
        )

    def number_of():
        used.append(len(used))
        return used[-1]

    barrier = pltpu.get_barrier_semaphore()
    far_z = (1, depth - 1, 2, depth - 2, RING, depth - RING, 2 * RING)
    for dz in far_z:
        pl.semaphore_signal(barrier, inc=1, device_id=deep(dz), device_id_type=MESH)

    @pl.loop(1, PEERS)
    def _(i):
        pl.semaphore_signal(barrier, inc=1, device_id=(ctx, (exp + i) % PEERS), device_id_type=MESH)

    pl.semaphore_signal(barrier, inc=1, device_id=sibling, device_id_type=MESH)

    def row_features(yy):
        return pl.ds(pl.multiple_of(yy * wide, wide), wide)

    def features(j):
        return pl.ds(pl.multiple_of(j * f, f), f)

    quarter = hd // RING
    load_qw = pltpu.make_async_copy(query_weight.at[:, row_features(y)], qw.at[0], local.at[0])
    load_qw.start()

    def own_quarter():
        return output_weight.at[core, pl.ds(pl.multiple_of(r * quarter, quarter), quarter)]

    load_wout = pltpu.make_async_copy(own_quarter().at[:, features(exp)], wout.at[0, core, r], local.at[1])
    load_wout.start()

    tok[0] = tokens[...]
    kv_part[:, :hd] = dot(tokens[...], key_weight[...]).astype(jnp.bfloat16)
    kv_part[:, hd:] = dot(tokens[...], value_weight[...]).astype(jnp.bfloat16)

    column = lax.broadcasted_iota(jnp.int32, (128, t), 0)
    at = column // mine
    expert = ((((y + at // RING) % RING) * RING) + (x + at % RING) % RING) * mine + column % mine
    routed = jnp.zeros((128, t), jnp.float32)
    gate_sum = jnp.zeros((128, t), jnp.float32)
    for route in range(routes):
        hit = expert_ids[route : route + 1, :] == expert
        routed = jnp.where(hit, 1.0, routed)
        gate_sum = jnp.where(hit, gates[route : route + 1, :], gate_sum)
    earlier = jnp.where(
        lax.broadcasted_iota(jnp.int32, (t, t), 0) < lax.broadcasted_iota(jnp.int32, (t, t), 1), 1.0, 0.0
    ).astype(jnp.bfloat16)
    slot_row[...] = jnp.where(routed > 0.5, dot(routed.astype(jnp.bfloat16), earlier), -1.0)
    slot_of[...] = jnp.transpose(slot_row[...])
    gate_of[...] = jnp.transpose(gate_sum)

    pl.semaphore_wait(barrier, PEERS - 1 + len(far_z) + 1)

    kv_first = number_of()

    @pl.loop(1, PEERS)
    def _(i):
        j = (exp + i) % PEERS
        rows = pl.ds(pl.multiple_of(j * share, share), share)
        send(kv_part.at[rows], kv_in.at[i], (ctx, j), kv_first).start()

    qw_moves = {
        dy: send(
            query_weight.at[core, row_features((y + dy) % RING)], qw.at[RING - dy, core], place(dy, 0)
        )
        for dy in (1, 3, 2)
    }
    half = t // 2
    tok_moves = {
        3: send(tok.at[0], tok.at[3], place(0, 1)),
        1: send(tok.at[0], tok.at[1], place(0, 3)),
        "2a": send(tok.at[3, pl.ds(0, half)], tok.at[2, pl.ds(0, half)], place(0, 1)),
        "2b": send(tok.at[1, pl.ds(half, half)], tok.at[2, pl.ds(half, half)], place(0, 3)),
    }
    for move in (qw_moves[2], tok_moves[1], tok_moves[3], qw_moves[1], qw_moves[3]):
        move.start()

    w_first = number_of()

    def send_wout():
        @pl.loop(1, PEERS)
        def _(i):
            dy, dx = i // RING, i % RING
            j = ((y + dy) % RING) * RING + (x + dx) % RING
            back = ((RING - dy) % RING) * RING + (RING - dx) % RING
            send(own_quarter().at[:, features(j)], wout.at[back, core, r], (ctx, j), w_first).start()

    send_wout()

    drain(kv_in.at[pl.ds(1, PEERS - 1)], recv_sem.at[kv_first])
    summed = kv_part[pl.ds(pl.multiple_of(exp * share, share), share)].astype(jnp.float32)
    for i in range(1, PEERS):
        summed += kv_in[i].astype(jnp.float32)
    kv[m, r, core, x] = summed.astype(jnp.bfloat16)
    stride_moves = [
        send(kv.at[m, r, core, x], kv.at[m, r, core, x], deep(dz)) for dz in (2 * RING, RING, 3 * RING)
    ]
    for move in stride_moves:
        move.start()
    m4, m8, m12 = (m + 1) % RING, (m + 2) % RING, (m + 3) % RING

    def got(piece, move_number):
        return send(piece, piece, sibling, move_number)

    first_of_stride = used[-3]
    stride_in = [
        got(kv.at[mm, r, core, x], first_of_stride + n) for n, mm in enumerate((m8, m12, m4))
    ]

    r1, r2, r3 = (r + 1) % RING, (r + 2) % RING, (r + 3) % RING
    low_m, high_m = pl.ds(0, RING // 2), pl.ds(RING // 2, RING // 2)
    residue_moves = [
        send(kv.at[low_m, r, core, x], kv.at[low_m, r, core, x], deep(2)),
        send(kv.at[high_m, r, core, x], kv.at[high_m, r, core, x], deep(depth - 2)),
        send(kv.at[:, r, core, x], kv.at[:, r, core, x], deep(1)),
        send(kv.at[:, r, core, x], kv.at[:, r, core, x], deep(depth - 1)),
    ]
    first_of_residue = used[-4]
    residue_in = [
        got(kv.at[low_m, r2, core, x], first_of_residue),
        got(kv.at[high_m, r2, core, x], first_of_residue + 1),
        got(kv.at[:, r3, core, x], first_of_residue + 2),
        got(kv.at[:, r1, core, x], first_of_residue + 3),
    ]
    x1, x2, x3 = (x + 1) % RING, (x + 2) % RING, (x + 3) % RING
    x_numbers = {step: number_of() for step in (1, 3, 2)}
    x_moves = []

    def push_along_x(rr):
        for step in (1, 3, 2):
            piece = kv.at[:, rr, core, x]
            x_moves.append(send(piece, piece, place(0, step), x_numbers[step]))
            x_moves[-1].start()

    columns = (x, x3, x1, x2)
    across = [send(kv.at[:, :, core, xx], kv.at[:, :, core, xx], sibling) for xx in columns]
    first_across = used[-4]
    across_in = [got(kv.at[:, :, other_core, xx], first_across + n) for n, xx in enumerate(columns)]

    position = lax.broadcasted_iota(jnp.int32, (t, 128), 0)
    high = (position // 16).astype(jnp.float32).astype(jnp.bfloat16)
    low = (position % 16).astype(jnp.float32).astype(jnp.bfloat16)
    place_of = jnp.concatenate([high, low], axis=1)
    slots = lax.broadcasted_iota(jnp.int32, (capacity, t), 0).astype(jnp.float32)
    for n in range(RING * mine):
        line = (n // mine) * (RING * mine) + n % mine
        pick[n] = jnp.where(slot_row[line : line + 1, :] == slots, 1.0, 0.0).astype(jnp.bfloat16)
        found = dot(pick[n], place_of)
        where_row[n] = 16.0 * found[:, :128] + found[:, 128:]

    tok_moves[3].wait_recv()
    tok_moves["2a"].start()
    tok_moves[1].wait_recv()
    tok_moves["2b"].start()

    for move in stride_in:
        move.wait_recv()
    for move in residue_moves:
        move.start()
    push_along_x(r)

    pieces = PlaneGather.order()

    def fill_spread(begin, end):
        lanes = lax.broadcasted_iota(jnp.int32, (t, LANES), 1).astype(jnp.float32)
        for p in range(begin, end):
            part, slot = pieces[p]
            n = slot * mine + part
            spread[:, p * LANES : (p + 1) * LANES] = jnp.where(
                slot_of[:, n : n + 1] == lanes, gate_of[:, n : n + 1], 0.0
            ).astype(jnp.bfloat16)

    fill_spread(0, 8)
    residue_in[2].wait_recv()
    push_along_x(r3)
    residue_in[3].wait_recv()
    push_along_x(r1)
    residue_in[0].wait_recv()
    residue_in[1].wait_recv()
    push_along_x(r2)
    across[0].start()
    fill_spread(8, 12)
    load_wout.wait()
    drain(wout.at[pl.ds(1, PEERS - 1), core, r], recv_sem.at[w_first])
    low_s, high_s = pl.ds(0, PEERS // 2), pl.ds(PEERS // 2, PEERS // 2)
    w_moves = [
        send(wout.at[low_s, core, r], wout.at[low_s, core, r], deep(2)),
        send(wout.at[high_s, core, r], wout.at[high_s, core, r], deep(depth - 2)),
        send(wout.at[:, core, r], wout.at[:, core, r], deep(1)),
        send(wout.at[:, core, r], wout.at[:, core, r], deep(depth - 1)),
    ]
    first_of_w = used[-4]
    w_in = [
        got(wout.at[low_s, core, r2], first_of_w),
        got(wout.at[high_s, core, r2], first_of_w + 1),
        got(wout.at[:, core, r3], first_of_w + 2),
        got(wout.at[:, core, r1], first_of_w + 3),
    ]
    for move in w_moves:
        move.start()

    fill_spread(12, 16)


    qw_across, qw_across_in = {}, {}
    for dy in (1, 3, 2):
        slot = RING - dy
        qw_moves[dy].wait_recv()
        qw_across[slot] = send(qw.at[slot, core], qw.at[slot, core], sibling)
        qw_across_in[slot] = got(qw.at[slot, other_core], used[-1])
        qw_across[slot].start()

    tok_moves["2a"].wait_recv()
    tok_moves["2b"].wait_recv()

    def partial_queries(dy):
        for part in range(2):
            rows = pl.ds(part * half, half)
            acc = jnp.zeros((half, mine * hd), jnp.float32)
            for dx in range(RING):
                own = features((x + dx) % RING)
                weight = jnp.concatenate([qw[dy, a, own] for a in range(mine)], axis=1)
                acc += dot(tok[dx, rows], weight)
            q_dense[rows] = acc.astype(jnp.bfloat16)
        for a in range(mine):
            q_part[dy, pl.ds(a * capacity, capacity)] = dot(
                pick[dy * mine + a], q_dense[:, a * hd : (a + 1) * hd]
            ).astype(jnp.bfloat16)

    q_part_moves = {
        dy: send(q_part.at[dy], q_part.at[2 * RING - dy], place(dy, 0)) for dy in range(1, RING)
    }
    load_qw.wait()
    for dy in (3, 1, 2):
        qw_across_in[dy].wait_recv()
        partial_queries(dy)
        q_part_moves[dy].start()
    partial_queries(0)

    fill_spread(16, 2 * PEERS)
    for n, step in enumerate((1, 3, 2)):
        drain(kv.at[:, :, core, columns[n + 1]], recv_sem.at[x_numbers[step]])
        across[n + 1].start()

    for dy in (3, 1, 2):
        q_part_moves[dy].wait_recv()
    q_all[0] = functools.reduce(
        jnp.add, [q_part[s].astype(jnp.float32) for s in (0, 5, 6, 7)]
    ).astype(jnp.bfloat16)
    q_moves = {dy: send(q_all.at[0], q_all.at[RING - dy], place(dy, 0)) for dy in range(1, RING)}
    for dy in (2, 1, 3):
        q_moves[dy].start()

    for move in across_in:
        move.wait_recv()

    factor = math.log2(math.e) / math.sqrt(hd)
    groups = z // 4
    span = RING * share
    block = 8 * span

    def attend(dy):
        top_score[...] = jnp.full_like(top_score, LOWEST)
        num[...] = jnp.zeros_like(num)

        def step(g, masked):
            keys = kv[g].reshape(block, 2 * hd)
            values = jnp.concatenate([keys[:, hd:], jnp.ones((block, hd), jnp.bfloat16)], axis=1)
            keys = keys[:, :hd]
            for a in range(mine):
                rows = pl.ds(a * capacity, capacity)
                scores = nt_dot(q_all[dy, rows], keys)
                if masked:
                    index = lax.broadcasted_iota(jnp.int32, (1, block), 1)
                    at = (8 * g + index // span - ctx) * t + y * span + index % span
                    scores = jnp.where(
                        at.astype(jnp.float32) <= where_row[dy * mine + a][:, 0:1], scores, LOWEST
                    )
                before = top_score[rows, 0:1]
                now = jnp.maximum(before, jnp.max(scores, axis=1, keepdims=True))
                weights = jnp.exp2((scores - now) * factor).astype(jnp.bfloat16)
                num[rows] = num[rows] * jnp.exp2((before - now) * factor) + dot(weights, values)
                top_score[rows] = jnp.broadcast_to(now, (capacity, 128))

        @pl.loop(0, groups)
        def _(g):
            step(g, False)

        step(groups, True)
        for a in range(mine):
            rows = pl.ds(a * capacity, capacity)
            norm = num[rows, hd:]
            part_out[dy, rows] = (num[rows, :hd] / norm).astype(jnp.bfloat16)
            lse = top_score[rows, 0:1] * factor + jnp.log2(norm[:, 0:1])
            part_lse[dy, pl.ds(a * 8, 8)] = to_row(lse)

    def diagonal():
        return lax.broadcasted_iota(jnp.int32, (capacity, LANES), 0) == lax.broadcasted_iota(
            jnp.int32, (capacity, LANES), 1
        )

    def to_row(values):
        row = jnp.sum(jnp.where(diagonal(), values, 0.0), axis=0, keepdims=True)
        return jnp.broadcast_to(row, (8, LANES))

    def to_column(row):
        return jnp.sum(jnp.where(diagonal(), row, 0.0), axis=1, keepdims=True)

    moves = []
    for dy in (0, 1, 3, 2):
        if dy:
            q_moves[RING - dy].wait_recv()
        attend(dy)
        if dy:
            moves.append(send(part_out.at[dy], part_out.at[2 * RING - dy], place(dy, 0)))
            moves.append(send(part_lse.at[dy], part_lse.at[2 * RING - dy], place(dy, 0)))
            moves[-2].start()
            moves[-1].start()
        if dy == 0:
            for move in w_in:
                move.wait_recv()
            w_across = send(wout.at[:, core], wout.at[:, core], sibling)
            w_across_in = got(wout.at[:, other_core], used[-1])
            w_across.start()

    produced[...] = jnp.zeros_like(produced)
    for move in moves:
        move.wait_recv()
    for a in range(mine):
        rows = pl.ds(a * capacity, capacity)
        parts = (0, 5, 6, 7)
        lses = [to_column(part_lse[s, pl.ds(a * 8, 1)]) for s in parts]
        top = functools.reduce(jnp.maximum, lses)
        weights = [jnp.exp2(lse - top) for lse in lses]
        norm = functools.reduce(jnp.add, weights)
        rows_sum = functools.reduce(
            jnp.add, [w * part_out[s, rows].astype(jnp.float32) for w, s in zip(weights, parts)]
        )
        heads[0, rows] = (rows_sum / norm).astype(jnp.bfloat16)

    seen = []

    def make_output(part, slot):
        begin = len(seen) * LANES
        seen.append((part, slot))
        made = dot(heads[slot, pl.ds(part * capacity, capacity)], wout[slot, part].reshape(hd, f))
        produced[begin : begin + capacity] = made.astype(jnp.bfloat16)

    added = [0]

    def beside(stage):
        if stage == 0:
            w_across_in.wait_recv()
        else:
            begin, end = added[0] * LANES, len(seen) * LANES
            part = dot(spread[:, begin:end], produced[begin:end])
            if stage == 1:
                total[...] = part
            elif stage < 4:
                total[...] += part
            else:
                out[...] = (total[...] + part).astype(jnp.bfloat16)
            added[0] = len(seen)

    head_gather = PlaneGather(heads, mine * capacity, head_send, head_recv, place)
    head_gather.run(make_output, beside)
    assert seen == pieces

    for step in (1, 3, 2):
        drain(kv.at[:, :, core, x], send_sem.at[x_numbers[step]])
    head_gather.finish()
    drain(kv_in.at[pl.ds(1, PEERS - 1)], send_sem.at[kv_first])
    drain(wout.at[pl.ds(1, PEERS - 1), core, r], send_sem.at[w_first])
    for copy in (
        *qw_moves.values(),
        *tok_moves.values(),
        *stride_moves,
        *residue_moves,
        *across,
        *w_moves,
        *qw_across.values(),
        *q_part_moves.values(),
        *q_moves.values(),
        *moves,
        w_across,
    ):
        copy.wait_send()


def per_device(depth, tokens, expert_ids, gates, query_weight, key_weight, value_weight, output_weight):
    t, f = tokens.shape
    routes = expert_ids.shape[1]
    mine, model, hd = query_weight.shape
    experts = mine * PEERS
    capacity = min(t, max(2, 5 * t * routes // (4 * experts)))
    owned = mine * capacity
    share = t // PEERS
    bf16, f32 = jnp.bfloat16, jnp.float32
    vmem, anywhere = pl.BlockSpec(memory_space=pltpu.VMEM), pl.BlockSpec(memory_space=pl.ANY)
    return pl.pallas_call(
        functools.partial(layer, capacity, depth),
        out_shape=jax.ShapeDtypeStruct((t, f), bf16),
        in_specs=[vmem, vmem, vmem, anywhere, vmem, vmem, anywhere],
        out_specs=vmem,
        scratch_shapes=[
            pltpu.VMEM((RING, t, f), bf16),
            pltpu.VMEM((RING, mine, RING * f, hd), bf16),
            pltpu.VMEM((t, 2 * hd), bf16),
            pltpu.VMEM((PEERS, share, 2 * hd), bf16),
            pltpu.VMEM((depth // RING, RING, 2, RING, share, 2 * hd), bf16),
            pltpu.VMEM((t, mine * hd), bf16),
            pltpu.VMEM((2 * RING, owned, hd), bf16),
            pltpu.VMEM((RING, owned, hd), bf16),
            pltpu.VMEM((t, 128), f32),
            pltpu.VMEM((t, 128), f32),
            pltpu.VMEM((128, t), f32),
            pltpu.VMEM((t, experts * LANES), bf16),
            pltpu.VMEM((RING * mine, capacity, t), bf16),
            pltpu.VMEM((RING * mine, capacity, 128), f32),
            pltpu.VMEM((PEERS, mine, RING, hd // RING, f), bf16),
            pltpu.VMEM((owned, 128), f32),
            pltpu.VMEM((owned, 2 * hd), f32),
            pltpu.VMEM((2 * RING, owned, hd), bf16),
            pltpu.VMEM((2 * RING, 8 * mine, LANES), f32),
            pltpu.VMEM((PEERS, owned, hd), bf16),
            pltpu.VMEM((experts * LANES, f), bf16),
            pltpu.VMEM((t, f), f32),
            pltpu.SemaphoreType.DMA((40,)),
            pltpu.SemaphoreType.DMA((40,)),
            pltpu.SemaphoreType.DMA((64,)),
            pltpu.SemaphoreType.DMA((64,)),
            pltpu.SemaphoreType.DMA((2,)),
        ],
        compiler_params=pltpu.CompilerParams(
            collective_id=0, has_side_effects=True, vmem_limit_bytes=56 * 1024 * 1024
        ),
    )(tokens, expert_ids.T, gates.T, query_weight, key_weight, value_weight, output_weight)


def solution(mesh):
    in_specs = (
        P("ctx", "exp"),
        P("ctx", None),
        P("ctx", None),
        P("exp", None, None),
        P("exp", None),
        P("exp", None),
        P("exp", None, None),
    )
    out_specs = P("ctx", "exp")
    return jax.shard_map(
        functools.partial(per_device, mesh.shape["ctx"] // 2),
        mesh=mesh,
        in_specs=in_specs,
        out_specs=out_specs,
        check_vma=False,
    )
```

```python
import functools
import math

import jax
import jax.numpy as jnp
from jax import lax
from jax.experimental import pallas as pl
from jax.experimental.pallas import tpu as pltpu
from jax.sharding import PartitionSpec as P

MESH = pl.DeviceIdType.MESH
RING = 4
PEERS = RING * RING
LANES = 256
LOWEST = -1e30


def nt_dot(a, b):
    return lax.dot_general(a, b, (((1,), (1,)), ((), ())), preferred_element_type=jnp.float32)


def tn_dot(a, b):
    return lax.dot_general(a, b, (((0,), (0,)), ((), ())), preferred_element_type=jnp.float32)


def dot(a, b):
    return jnp.dot(a, b, preferred_element_type=jnp.float32)


def drain(ref, sem):
    pltpu.make_async_copy(ref, ref, sem).wait()


class PlaneGather:
    STEPS = {3: 1, 1: 3, 2: 2}

    def __init__(self, buf, rows, send_sem, recv_sem, place):
        self.buf, self.rows = buf, rows // 2
        self.send_sem, self.recv_sem, self.place = send_sem, recv_sem, place
        self.started = []

    @staticmethod
    def slot(half, first, second):
        return second * RING + first if half == 0 else first * RING + second

    @staticmethod
    def order():
        slot = PlaneGather.slot
        pieces = [(half, slot(half, first, 0)) for first in (0, 3, 1, 2) for half in range(2)]
        pieces += [
            (half, slot(half, first, second)) for first in (0, 3, 1, 2) for second in (3, 1, 2) for half in range(2)
        ]
        return pieces

    def message(self, half, phase, other, where):
        number = half * PEERS + (where * RING if phase == 0 else other * RING + where)
        rows = pl.ds(half * self.rows, self.rows)
        if phase == 0:
            src, dst = self.slot(half, 0, 0), self.slot(half, where, 0)
        else:
            src, dst = self.slot(half, other, 0), self.slot(half, other, where)
        step = self.STEPS[where]
        along_x = (half == 0) == (phase == 0)
        return pltpu.make_async_remote_copy(
            src_ref=self.buf.at[src, rows],
            dst_ref=self.buf.at[dst, rows],
            send_sem=self.send_sem.at[number],
            recv_sem=self.recv_sem.at[number],
            device_id=self.place(0, step) if along_x else self.place(step, 0),
            device_id_type=MESH,
        )

    def start(self, *key):
        copy = self.message(*key)
        copy.start()
        self.started.append(copy)

    def wait(self, *key):
        self.message(*key).wait_recv()

    def finish(self):
        for copy in self.started:
            copy.wait_send()

    def run(self, arrived, beside):
        for where in (3, 1, 2):
            for half in range(2):
                self.start(half, 0, 0, where)
        for where in (3, 1, 2):
            for half in range(2):
                self.start(half, 1, 0, where)
        beside(0)
        for half in range(2):
            arrived(half, 0)
        for first in (3, 1, 2):
            for half in range(2):
                self.wait(half, 0, 0, first)
                for where in (3, 1, 2):
                    self.start(half, 1, first, where)
        for first in (3, 1, 2):
            for half in range(2):
                arrived(half, self.slot(half, first, 0))
        for first in (0, 3, 1, 2):
            for where in (3, 1, 2):
                for half in range(2):
                    self.wait(half, 1, first, where)
                    arrived(half, self.slot(half, first, where))
            beside({0: 1, 3: 2, 1: 3, 2: 4}[first])


def layer(
    capacity,
    depth,
    tokens,
    expert_ids,
    gates,
    query_weight,
    key_weight,
    value_weight,
    output_weight,
    out,
    tok,
    qw,
    kv_part,
    kv_in,
    kv,
    q_dense,
    q_part,
    q_all,
    slot_of,
    gate_of,
    slot_row,
    spread,
    pick,
    where_row,
    wout,
    top_score,
    num,
    part_out,
    part_lse,
    heads,
    produced,
    total,
    head_send,
    head_recv,
    send_sem,
    recv_sem,
    local,
):
    ctx, exp = lax.axis_index("ctx"), lax.axis_index("exp")
    y, x = exp // RING, exp % RING
    z, core = ctx // 2, ctx % 2
    m, r = z // RING, z % RING
    other_core = 1 - core
    t, f = tokens.shape
    routes = expert_ids.shape[0]
    mine = query_weight.shape[0]
    hd = query_weight.shape[2]
    share = t // PEERS
    wide = RING * f

    def place(dy, dx):
        return (ctx, ((y + dy) % RING) * RING + (x + dx) % RING)

    def deep(dz):
        return (((z + dz) % depth) * 2 + core, exp)

    sibling = (ctx + 1 - 2 * core, exp)
    used = []

    def send(src, dst, device, number=None):
        if number is None:
            number = len(used)
            used.append(number)
        return pltpu.make_async_remote_copy(
            src_ref=src,
            dst_ref=dst,
            send_sem=send_sem.at[number],
            recv_sem=recv_sem.at[number],
            device_id=device,
            device_id_type=MESH,
        )

    def number_of():
        used.append(len(used))
        return used[-1]

    barrier = pltpu.get_barrier_semaphore()
    far_z = (1, depth - 1, 2, depth - 2, RING, depth - RING, 2 * RING)
    for dz in far_z:
        pl.semaphore_signal(barrier, inc=1, device_id=deep(dz), device_id_type=MESH)

    @pl.loop(1, PEERS)
    def _(i):
        pl.semaphore_signal(barrier, inc=1, device_id=(ctx, (exp + i) % PEERS), device_id_type=MESH)

    pl.semaphore_signal(barrier, inc=1, device_id=sibling, device_id_type=MESH)

    def row_features(yy):
        return pl.ds(pl.multiple_of(yy * wide, wide), wide)

    def features(j):
        return pl.ds(pl.multiple_of(j * f, f), f)

    quarter = hd // RING
    load_qw = pltpu.make_async_copy(query_weight.at[:, row_features(y)], qw.at[0], local.at[0])
    load_qw.start()

    def own_quarter():
        return output_weight.at[core, pl.ds(pl.multiple_of(r * quarter, quarter), quarter)]

    load_wout = pltpu.make_async_copy(own_quarter().at[:, features(exp)], wout.at[0, core, r], local.at[1])
    load_wout.start()

    tok[0] = tokens[...]
    kv_part[:, :hd] = dot(tokens[...], key_weight[...]).astype(jnp.bfloat16)
    kv_part[:, hd:] = dot(tokens[...], value_weight[...]).astype(jnp.bfloat16)

    column = lax.broadcasted_iota(jnp.int32, (128, t), 0)
    at = column // mine
    expert = ((((y + at // RING) % RING) * RING) + (x + at % RING) % RING) * mine + column % mine
    routed = jnp.zeros((128, t), jnp.float32)
    gate_sum = jnp.zeros((128, t), jnp.float32)
    for route in range(routes):
        hit = expert_ids[route : route + 1, :] == expert
        routed = jnp.where(hit, 1.0, routed)
        gate_sum = jnp.where(hit, gates[route : route + 1, :], gate_sum)
    earlier = jnp.where(
        lax.broadcasted_iota(jnp.int32, (t, t), 0) < lax.broadcasted_iota(jnp.int32, (t, t), 1), 1.0, 0.0
    ).astype(jnp.bfloat16)
    slot_row[...] = jnp.where(routed > 0.5, dot(routed.astype(jnp.bfloat16), earlier), -1.0)
    slot_of[...] = jnp.transpose(slot_row[...])
    gate_of[...] = jnp.transpose(gate_sum)

    pl.semaphore_wait(barrier, PEERS - 1 + len(far_z) + 1)

    kv_first = number_of()

    @pl.loop(1, PEERS)
    def _(i):
        j = (exp + i) % PEERS
        rows = pl.ds(pl.multiple_of(j * share, share), share)
        send(kv_part.at[rows], kv_in.at[i], (ctx, j), kv_first).start()

    qw_moves = {
        dy: send(
            query_weight.at[core, row_features((y + dy) % RING)], qw.at[RING - dy, core], place(dy, 0)
        )
        for dy in (1, 3)
    }
    part = pl.ds(pl.multiple_of(r * f, f), f)
    far_quarter = pl.ds(pl.multiple_of(((y + 2) % RING) * wide + r * f, f), f)
    qw_moves[2] = send(query_weight.at[core, far_quarter], qw.at[2, core, part], place(2, 0))
    half = t // 2
    tok_moves = {
        3: send(tok.at[0], tok.at[3], place(0, 1)),
        1: send(tok.at[0], tok.at[1], place(0, 3)),
        "2a": send(tok.at[3, pl.ds(0, half)], tok.at[2, pl.ds(0, half)], place(0, 1)),
        "2b": send(tok.at[1, pl.ds(half, half)], tok.at[2, pl.ds(half, half)], place(0, 3)),
    }
    for move in (qw_moves[2], tok_moves[1], tok_moves[3], qw_moves[1], qw_moves[3]):
        move.start()

    w_first = number_of()

    def send_wout():
        @pl.loop(1, PEERS)
        def _(i):
            dy, dx = i // RING, i % RING
            j = ((y + dy) % RING) * RING + (x + dx) % RING
            back = ((RING - dy) % RING) * RING + (RING - dx) % RING
            send(own_quarter().at[:, features(j)], wout.at[back, core, r], (ctx, j), w_first).start()

    send_wout()

    drain(kv_in.at[pl.ds(1, PEERS - 1)], recv_sem.at[kv_first])
    summed = kv_part[pl.ds(pl.multiple_of(exp * share, share), share)].astype(jnp.float32)
    for i in range(1, PEERS):
        summed += kv_in[i].astype(jnp.float32)
    kv[m, r, core, x] = summed.astype(jnp.bfloat16)
    stride_moves = [
        send(kv.at[m, r, core, x], kv.at[m, r, core, x], deep(dz)) for dz in (2 * RING, RING, 3 * RING)
    ]
    for move in stride_moves:
        move.start()
    m4, m8, m12 = (m + 1) % RING, (m + 2) % RING, (m + 3) % RING

    def got(piece, move_number):
        return send(piece, piece, sibling, move_number)

    first_of_stride = used[-3]
    stride_in = [
        got(kv.at[mm, r, core, x], first_of_stride + n) for n, mm in enumerate((m8, m12, m4))
    ]

    r1, r2, r3 = (r + 1) % RING, (r + 2) % RING, (r + 3) % RING

    def far_part(rr, begin, rows):
        return qw.at[2, core, pl.ds(pl.multiple_of(rr * f + begin, f // 2), rows)]

    far_moves = [
        send(far_part(r, 0, f // 2), far_part(r, 0, f // 2), deep(2)),
        send(far_part(r, f // 2, f // 2), far_part(r, f // 2, f // 2), deep(depth - 2)),
        send(far_part(r, 0, f), far_part(r, 0, f), deep(1)),
        send(far_part(r, 0, f), far_part(r, 0, f), deep(depth - 1)),
    ]
    first_of_far = used[-4]
    far_in = [
        got(far_part(r2, 0, f // 2), first_of_far),
        got(far_part(r2, f // 2, f // 2), first_of_far + 1),
        got(far_part(r3, 0, f), first_of_far + 2),
        got(far_part(r1, 0, f), first_of_far + 3),
    ]
    qw_moves[2].wait_recv()
    for move in far_moves:
        move.start()

    tok_moves[3].wait_recv()
    tok_moves["2a"].start()
    tok_moves[1].wait_recv()
    tok_moves["2b"].start()

    low_m, high_m = pl.ds(0, RING // 2), pl.ds(RING // 2, RING // 2)
    residue_moves = [
        send(kv.at[low_m, r, core, x], kv.at[low_m, r, core, x], deep(2)),
        send(kv.at[high_m, r, core, x], kv.at[high_m, r, core, x], deep(depth - 2)),
        send(kv.at[:, r, core, x], kv.at[:, r, core, x], deep(1)),
        send(kv.at[:, r, core, x], kv.at[:, r, core, x], deep(depth - 1)),
    ]
    first_of_residue = used[-4]
    residue_in = [
        got(kv.at[low_m, r2, core, x], first_of_residue),
        got(kv.at[high_m, r2, core, x], first_of_residue + 1),
        got(kv.at[:, r3, core, x], first_of_residue + 2),
        got(kv.at[:, r1, core, x], first_of_residue + 3),
    ]
    x1, x2, x3 = (x + 1) % RING, (x + 2) % RING, (x + 3) % RING
    x_numbers = {step: number_of() for step in (1, 3, 2)}
    x_moves = []

    def push_along_x(rr):
        for step in (1, 3, 2):
            piece = kv.at[:, rr, core, x]
            x_moves.append(send(piece, piece, place(0, step), x_numbers[step]))
            x_moves[-1].start()

    columns = (x, x3, x1, x2)
    across = [send(kv.at[:, :, core, xx], kv.at[:, :, core, xx], sibling) for xx in columns]
    first_across = used[-4]
    across_in = [got(kv.at[:, :, other_core, xx], first_across + n) for n, xx in enumerate(columns)]

    position = lax.broadcasted_iota(jnp.int32, (t, 128), 0)
    high = (position // 16).astype(jnp.float32).astype(jnp.bfloat16)
    low = (position % 16).astype(jnp.float32).astype(jnp.bfloat16)
    place_of = jnp.concatenate([high, low], axis=1)
    slots = lax.broadcasted_iota(jnp.int32, (capacity, t), 0).astype(jnp.float32)
    for n in range(RING * mine):
        line = (n // mine) * (RING * mine) + n % mine
        pick[n] = jnp.where(slot_row[line : line + 1, :] == slots, 1.0, 0.0).astype(jnp.bfloat16)
        found = dot(pick[n], place_of)
        where_row[n] = 16.0 * found[:, :128] + found[:, 128:]

    for move in stride_in:
        move.wait_recv()
    for move in residue_moves:
        move.start()
    push_along_x(r)

    pieces = PlaneGather.order()

    def fill_spread(begin, end):
        lanes = lax.broadcasted_iota(jnp.int32, (t, LANES), 1).astype(jnp.float32)
        for p in range(begin, end):
            part, slot = pieces[p]
            n = slot * mine + part
            spread[:, p * LANES : (p + 1) * LANES] = jnp.where(
                slot_of[:, n : n + 1] == lanes, gate_of[:, n : n + 1], 0.0
            ).astype(jnp.bfloat16)

    fill_spread(0, 8)
    residue_in[2].wait_recv()
    push_along_x(r3)
    residue_in[3].wait_recv()
    push_along_x(r1)
    residue_in[0].wait_recv()
    residue_in[1].wait_recv()
    push_along_x(r2)
    across[0].start()
    fill_spread(8, 12)
    load_wout.wait()
    drain(wout.at[pl.ds(1, PEERS - 1), core, r], recv_sem.at[w_first])
    low_s, high_s = pl.ds(0, PEERS // 2), pl.ds(PEERS // 2, PEERS // 2)
    w_moves = [
        send(wout.at[low_s, core, r], wout.at[low_s, core, r], deep(2)),
        send(wout.at[high_s, core, r], wout.at[high_s, core, r], deep(depth - 2)),
        send(wout.at[:, core, r], wout.at[:, core, r], deep(1)),
        send(wout.at[:, core, r], wout.at[:, core, r], deep(depth - 1)),
    ]
    first_of_w = used[-4]
    w_in = [
        got(wout.at[low_s, core, r2], first_of_w),
        got(wout.at[high_s, core, r2], first_of_w + 1),
        got(wout.at[:, core, r3], first_of_w + 2),
        got(wout.at[:, core, r1], first_of_w + 3),
    ]
    for move in w_moves:
        move.start()

    fill_spread(12, 16)


    qw_across, qw_across_in = {}, {}
    for dy in (1, 3, 2):
        slot = RING - dy
        for move in far_in if dy == 2 else [qw_moves[dy]]:
            move.wait_recv()
        qw_across[slot] = send(qw.at[slot, core], qw.at[slot, core], sibling)
        qw_across_in[slot] = got(qw.at[slot, other_core], used[-1])
        qw_across[slot].start()

    tok_moves["2a"].wait_recv()
    tok_moves["2b"].wait_recv()

    def partial_queries(dy):
        for part in range(2):
            rows = pl.ds(part * half, half)
            acc = jnp.zeros((half, mine * hd), jnp.float32)
            for dx in range(RING):
                own = features((x + dx) % RING)
                weight = jnp.concatenate([qw[dy, a, own] for a in range(mine)], axis=1)
                acc += dot(tok[dx, rows], weight)
            q_dense[rows] = acc.astype(jnp.bfloat16)
        for a in range(mine):
            q_part[dy, pl.ds(a * capacity, capacity)] = dot(
                pick[dy * mine + a], q_dense[:, a * hd : (a + 1) * hd]
            ).astype(jnp.bfloat16)

    q_part_moves = {
        dy: send(q_part.at[dy], q_part.at[2 * RING - dy], place(dy, 0)) for dy in range(1, RING)
    }
    for dy in (3, 1, 2):
        qw_across_in[dy].wait_recv()
        partial_queries(dy)
        q_part_moves[dy].start()
    load_qw.wait()
    partial_queries(0)

    fill_spread(16, 2 * PEERS)
    for n, step in enumerate((1, 3, 2)):
        drain(kv.at[:, :, core, columns[n + 1]], recv_sem.at[x_numbers[step]])
        across[n + 1].start()

    for dy in (3, 1, 2):
        q_part_moves[dy].wait_recv()
    q_all[0] = functools.reduce(
        jnp.add, [q_part[s].astype(jnp.float32) for s in (0, 5, 6, 7)]
    ).astype(jnp.bfloat16)
    q_moves = {dy: send(q_all.at[0], q_all.at[RING - dy], place(dy, 0)) for dy in range(1, RING)}
    for dy in (2, 1, 3):
        q_moves[dy].start()

    for move in across_in:
        move.wait_recv()

    factor = math.log2(math.e) / math.sqrt(hd)
    groups = z // 4
    span = RING * share
    block = 8 * span

    def attend(dy):
        top_score[...] = jnp.full_like(top_score, LOWEST)
        num[...] = jnp.zeros_like(num)

        def step(g, masked):
            keys = kv[g].reshape(block, 2 * hd)
            values = jnp.concatenate([keys[:, hd:], jnp.ones((block, hd), jnp.bfloat16)], axis=1)
            keys = keys[:, :hd]
            for a in range(mine):
                rows = pl.ds(a * capacity, capacity)
                scores = nt_dot(q_all[dy, rows], keys)
                if masked:
                    index = lax.broadcasted_iota(jnp.int32, (1, block), 1)
                    at = (8 * g + index // span - ctx) * t + y * span + index % span
                    scores = jnp.where(
                        at.astype(jnp.float32) <= where_row[dy * mine + a][:, 0:1], scores, LOWEST
                    )
                before = top_score[rows, 0:1]
                now = jnp.maximum(before, jnp.max(scores, axis=1, keepdims=True))
                weights = jnp.exp2((scores - now) * factor).astype(jnp.bfloat16)
                num[rows] = num[rows] * jnp.exp2((before - now) * factor) + dot(weights, values)
                top_score[rows] = jnp.broadcast_to(now, (capacity, 128))

        @pl.loop(0, groups)
        def _(g):
            step(g, False)

        step(groups, True)
        for a in range(mine):
            rows = pl.ds(a * capacity, capacity)
            norm = num[rows, hd:]
            part_out[dy, rows] = (num[rows, :hd] / norm).astype(jnp.bfloat16)
            lse = top_score[rows, 0:1] * factor + jnp.log2(norm[:, 0:1])
            part_lse[dy, pl.ds(a * 8, 8)] = to_row(lse)

    def diagonal():
        return lax.broadcasted_iota(jnp.int32, (capacity, LANES), 0) == lax.broadcasted_iota(
            jnp.int32, (capacity, LANES), 1
        )

    def to_row(values):
        row = jnp.sum(jnp.where(diagonal(), values, 0.0), axis=0, keepdims=True)
        return jnp.broadcast_to(row, (8, LANES))

    def to_column(row):
        return jnp.sum(jnp.where(diagonal(), row, 0.0), axis=1, keepdims=True)

    moves = []
    for dy in (0, 1, 3, 2):
        if dy:
            q_moves[RING - dy].wait_recv()
        attend(dy)
        if dy:
            moves.append(send(part_out.at[dy], part_out.at[2 * RING - dy], place(dy, 0)))
            moves.append(send(part_lse.at[dy], part_lse.at[2 * RING - dy], place(dy, 0)))
            moves[-2].start()
            moves[-1].start()
        if dy == 0:
            for move in w_in:
                move.wait_recv()
            w_across = send(wout.at[:, core], wout.at[:, core], sibling)
            w_across_in = got(wout.at[:, other_core], used[-1])
            w_across.start()

    produced[...] = jnp.zeros_like(produced)
    for move in moves:
        move.wait_recv()
    for a in range(mine):
        rows = pl.ds(a * capacity, capacity)
        parts = (0, 5, 6, 7)
        lses = [to_column(part_lse[s, pl.ds(a * 8, 1)]) for s in parts]
        top = functools.reduce(jnp.maximum, lses)
        weights = [jnp.exp2(lse - top) for lse in lses]
        norm = functools.reduce(jnp.add, weights)
        rows_sum = functools.reduce(
            jnp.add, [w * part_out[s, rows].astype(jnp.float32) for w, s in zip(weights, parts)]
        )
        heads[0, rows] = (rows_sum / norm).astype(jnp.bfloat16)

    seen = []

    def make_output(part, slot):
        begin = len(seen) * LANES
        seen.append((part, slot))
        made = dot(heads[slot, pl.ds(part * capacity, capacity)], wout[slot, part].reshape(hd, f))
        produced[begin : begin + capacity] = made.astype(jnp.bfloat16)

    added = [0]

    def beside(stage):
        if stage == 0:
            w_across_in.wait_recv()
        else:
            begin, end = added[0] * LANES, len(seen) * LANES
            part = dot(spread[:, begin:end], produced[begin:end])
            if stage == 1:
                total[...] = part
            elif stage < 4:
                total[...] += part
            else:
                out[...] = (total[...] + part).astype(jnp.bfloat16)
            added[0] = len(seen)

    head_gather = PlaneGather(heads, mine * capacity, head_send, head_recv, place)
    head_gather.run(make_output, beside)
    assert seen == pieces

    for step in (1, 3, 2):
        drain(kv.at[:, :, core, x], send_sem.at[x_numbers[step]])
    head_gather.finish()
    drain(kv_in.at[pl.ds(1, PEERS - 1)], send_sem.at[kv_first])
    drain(wout.at[pl.ds(1, PEERS - 1), core, r], send_sem.at[w_first])
    for copy in (
        *qw_moves.values(),
        *far_moves,
        *tok_moves.values(),
        *stride_moves,
        *residue_moves,
        *across,
        *w_moves,
        *qw_across.values(),
        *q_part_moves.values(),
        *q_moves.values(),
        *moves,
        w_across,
    ):
        copy.wait_send()


def per_device(depth, tokens, expert_ids, gates, query_weight, key_weight, value_weight, output_weight):
    t, f = tokens.shape
    routes = expert_ids.shape[1]
    mine, model, hd = query_weight.shape
    experts = mine * PEERS
    capacity = min(t, max(2, 5 * t * routes // (4 * experts)))
    owned = mine * capacity
    share = t // PEERS
    bf16, f32 = jnp.bfloat16, jnp.float32
    vmem, anywhere = pl.BlockSpec(memory_space=pltpu.VMEM), pl.BlockSpec(memory_space=pl.ANY)
    return pl.pallas_call(
        functools.partial(layer, capacity, depth),
        out_shape=jax.ShapeDtypeStruct((t, f), bf16),
        in_specs=[vmem, vmem, vmem, anywhere, vmem, vmem, anywhere],
        out_specs=vmem,
        scratch_shapes=[
            pltpu.VMEM((RING, t, f), bf16),
            pltpu.VMEM((RING, mine, RING * f, hd), bf16),
            pltpu.VMEM((t, 2 * hd), bf16),
            pltpu.VMEM((PEERS, share, 2 * hd), bf16),
            pltpu.VMEM((depth // RING, RING, 2, RING, share, 2 * hd), bf16),
            pltpu.VMEM((t, mine * hd), bf16),
            pltpu.VMEM((2 * RING, owned, hd), bf16),
            pltpu.VMEM((RING, owned, hd), bf16),
            pltpu.VMEM((t, 128), f32),
            pltpu.VMEM((t, 128), f32),
            pltpu.VMEM((128, t), f32),
            pltpu.VMEM((t, experts * LANES), bf16),
            pltpu.VMEM((RING * mine, capacity, t), bf16),
            pltpu.VMEM((RING * mine, capacity, 128), f32),
            pltpu.VMEM((PEERS, mine, RING, hd // RING, f), bf16),
            pltpu.VMEM((owned, 128), f32),
            pltpu.VMEM((owned, 2 * hd), f32),
            pltpu.VMEM((2 * RING, owned, hd), bf16),
            pltpu.VMEM((2 * RING, 8 * mine, LANES), f32),
            pltpu.VMEM((PEERS, owned, hd), bf16),
            pltpu.VMEM((experts * LANES, f), bf16),
            pltpu.VMEM((t, f), f32),
            pltpu.SemaphoreType.DMA((40,)),
            pltpu.SemaphoreType.DMA((40,)),
            pltpu.SemaphoreType.DMA((64,)),
            pltpu.SemaphoreType.DMA((64,)),
            pltpu.SemaphoreType.DMA((2,)),
        ],
        compiler_params=pltpu.CompilerParams(
            collective_id=0, has_side_effects=True, vmem_limit_bytes=56 * 1024 * 1024
        ),
    )(tokens, expert_ids.T, gates.T, query_weight, key_weight, value_weight, output_weight)


def solution(mesh):
    in_specs = (
        P("ctx", "exp"),
        P("ctx", None),
        P("ctx", None),
        P("exp", None, None),
        P("exp", None),
        P("exp", None),
        P("exp", None, None),
    )
    out_specs = P("ctx", "exp")
    return jax.shard_map(
        functools.partial(per_device, mesh.shape["ctx"] // 2),
        mesh=mesh,
        in_specs=in_specs,
        out_specs=out_specs,
        check_vma=False,
    )
```

```python
import functools
import math

import jax
import jax.numpy as jnp
from jax import lax
from jax.experimental import pallas as pl
from jax.experimental.pallas import tpu as pltpu
from jax.sharding import PartitionSpec as P

MESH = pl.DeviceIdType.MESH
RING = 4
PEERS = RING * RING
LANES = 256
LOWEST = -1e30


def nt_dot(a, b):
    return lax.dot_general(a, b, (((1,), (1,)), ((), ())), preferred_element_type=jnp.float32)


def tn_dot(a, b):
    return lax.dot_general(a, b, (((0,), (0,)), ((), ())), preferred_element_type=jnp.float32)


def dot(a, b):
    return jnp.dot(a, b, preferred_element_type=jnp.float32)


def drain(ref, sem):
    pltpu.make_async_copy(ref, ref, sem).wait()


class PlaneGather:
    STEPS = {3: 1, 1: 3, 2: 2}

    def __init__(self, buf, rows, send_sem, recv_sem, place):
        self.buf, self.rows = buf, rows // 2
        self.send_sem, self.recv_sem, self.place = send_sem, recv_sem, place
        self.started = []

    @staticmethod
    def slot(half, first, second):
        return second * RING + first if half == 0 else first * RING + second

    @staticmethod
    def order():
        slot = PlaneGather.slot
        pieces = [(half, slot(half, first, 0)) for first in (0, 3, 1, 2) for half in range(2)]
        pieces += [
            (half, slot(half, first, second)) for first in (0, 3, 1, 2) for second in (3, 1, 2) for half in range(2)
        ]
        return pieces

    def message(self, half, phase, other, where):
        number = half * PEERS + (where * RING if phase == 0 else other * RING + where)
        rows = pl.ds(half * self.rows, self.rows)
        if phase == 0:
            src, dst = self.slot(half, 0, 0), self.slot(half, where, 0)
        else:
            src, dst = self.slot(half, other, 0), self.slot(half, other, where)
        step = self.STEPS[where]
        along_x = (half == 0) == (phase == 0)
        return pltpu.make_async_remote_copy(
            src_ref=self.buf.at[src, rows],
            dst_ref=self.buf.at[dst, rows],
            send_sem=self.send_sem.at[number],
            recv_sem=self.recv_sem.at[number],
            device_id=self.place(0, step) if along_x else self.place(step, 0),
            device_id_type=MESH,
        )

    def start(self, *key):
        copy = self.message(*key)
        copy.start()
        self.started.append(copy)

    def wait(self, *key):
        self.message(*key).wait_recv()

    def finish(self):
        for copy in self.started:
            copy.wait_send()

    def run(self, arrived, beside):
        for where in (2, 3, 1):
            for half in range(2):
                self.start(half, 0, 0, where)
        for where in (3, 1, 2):
            for half in range(2):
                self.start(half, 1, 0, where)
        beside(0)
        for half in range(2):
            arrived(half, 0)
        for first in (3, 1, 2):
            for half in range(2):
                self.wait(half, 0, 0, first)
                for where in (2, 3, 1):
                    self.start(half, 1, first, where)
        for first in (3, 1, 2):
            for half in range(2):
                arrived(half, self.slot(half, first, 0))
        for first in (0, 3, 1, 2):
            for where in (3, 1, 2):
                for half in range(2):
                    self.wait(half, 1, first, where)
                    arrived(half, self.slot(half, first, where))
            beside({0: 1, 3: 2, 1: 3, 2: 4}[first])


def layer(
    capacity,
    depth,
    tokens,
    expert_ids,
    gates,
    query_weight,
    key_weight,
    value_weight,
    output_weight,
    out,
    tok,
    qw,
    kv_part,
    kv_in,
    kv,
    q_dense,
    q_part,
    q_all,
    slot_of,
    gate_of,
    slot_row,
    spread,
    pick,
    where_row,
    wout,
    top_score,
    num,
    part_out,
    part_lse,
    heads,
    produced,
    total,
    head_send,
    head_recv,
    send_sem,
    recv_sem,
    local,
):
    ctx, exp = lax.axis_index("ctx"), lax.axis_index("exp")
    y, x = exp // RING, exp % RING
    z, core = ctx // 2, ctx % 2
    m, r = z // RING, z % RING
    other_core = 1 - core
    t, f = tokens.shape
    routes = expert_ids.shape[0]
    mine = query_weight.shape[0]
    hd = query_weight.shape[2]
    share = t // PEERS
    wide = RING * f

    def place(dy, dx):
        return (ctx, ((y + dy) % RING) * RING + (x + dx) % RING)

    def deep(dz):
        return (((z + dz) % depth) * 2 + core, exp)

    sibling = (ctx + 1 - 2 * core, exp)
    used = []

    def send(src, dst, device, number=None):
        if number is None:
            number = len(used)
            used.append(number)
        return pltpu.make_async_remote_copy(
            src_ref=src,
            dst_ref=dst,
            send_sem=send_sem.at[number],
            recv_sem=recv_sem.at[number],
            device_id=device,
            device_id_type=MESH,
        )

    def number_of():
        used.append(len(used))
        return used[-1]

    barrier = pltpu.get_barrier_semaphore()
    far_z = (1, depth - 1, 2, depth - 2, RING, depth - RING, 2 * RING)
    for dz in far_z:
        pl.semaphore_signal(barrier, inc=1, device_id=deep(dz), device_id_type=MESH)

    @pl.loop(1, PEERS)
    def _(i):
        pl.semaphore_signal(barrier, inc=1, device_id=(ctx, (exp + i) % PEERS), device_id_type=MESH)

    pl.semaphore_signal(barrier, inc=1, device_id=sibling, device_id_type=MESH)

    def row_features(yy):
        return pl.ds(pl.multiple_of(yy * wide, wide), wide)

    def features(j):
        return pl.ds(pl.multiple_of(j * f, f), f)

    quarter = hd // RING
    load_qw = pltpu.make_async_copy(query_weight.at[:, row_features(y)], qw.at[0], local.at[0])
    load_qw.start()

    def own_quarter():
        return output_weight.at[core, pl.ds(pl.multiple_of(r * quarter, quarter), quarter)]

    load_wout = pltpu.make_async_copy(own_quarter().at[:, features(exp)], wout.at[0, core, r], local.at[1])
    load_wout.start()

    tok[0] = tokens[...]
    kv_part[:, :hd] = dot(tokens[...], key_weight[...]).astype(jnp.bfloat16)
    kv_part[:, hd:] = dot(tokens[...], value_weight[...]).astype(jnp.bfloat16)

    column = lax.broadcasted_iota(jnp.int32, (128, t), 0)
    at = column // mine
    expert = ((((y + at // RING) % RING) * RING) + (x + at % RING) % RING) * mine + column % mine
    routed = jnp.zeros((128, t), jnp.float32)
    gate_sum = jnp.zeros((128, t), jnp.float32)
    for route in range(routes):
        hit = expert_ids[route : route + 1, :] == expert
        routed = jnp.where(hit, 1.0, routed)
        gate_sum = jnp.where(hit, gates[route : route + 1, :], gate_sum)
    earlier = jnp.where(
        lax.broadcasted_iota(jnp.int32, (t, t), 0) < lax.broadcasted_iota(jnp.int32, (t, t), 1), 1.0, 0.0
    ).astype(jnp.bfloat16)
    slot_row[...] = jnp.where(routed > 0.5, dot(routed.astype(jnp.bfloat16), earlier), -1.0)
    slot_of[...] = jnp.transpose(slot_row[...])
    gate_of[...] = jnp.transpose(gate_sum)

    pl.semaphore_wait(barrier, PEERS - 1 + len(far_z) + 1)

    kv_first = number_of()

    @pl.loop(1, PEERS)
    def _(i):
        j = (exp + i) % PEERS
        rows = pl.ds(pl.multiple_of(j * share, share), share)
        send(kv_part.at[rows], kv_in.at[i], (ctx, j), kv_first).start()

    qw_moves = {
        dy: send(
            query_weight.at[core, row_features((y + dy) % RING)], qw.at[RING - dy, core], place(dy, 0)
        )
        for dy in (1, 3)
    }
    part = pl.ds(pl.multiple_of(r * f, f), f)
    far_quarter = pl.ds(pl.multiple_of(((y + 2) % RING) * wide + r * f, f), f)
    qw_moves[2] = send(query_weight.at[core, far_quarter], qw.at[2, core, part], place(2, 0))
    half = t // 2
    tok_moves = {
        3: send(tok.at[0], tok.at[3], place(0, 1)),
        1: send(tok.at[0], tok.at[1], place(0, 3)),
        "2a": send(tok.at[3, pl.ds(0, half)], tok.at[2, pl.ds(0, half)], place(0, 1)),
        "2b": send(tok.at[1, pl.ds(half, half)], tok.at[2, pl.ds(half, half)], place(0, 3)),
    }
    for move in (qw_moves[2], tok_moves[1], tok_moves[3], qw_moves[1], qw_moves[3]):
        move.start()

    w_first = number_of()

    def send_wout():
        @pl.loop(1, PEERS)
        def _(i):
            dy, dx = i // RING, i % RING
            j = ((y + dy) % RING) * RING + (x + dx) % RING
            back = ((RING - dy) % RING) * RING + (RING - dx) % RING
            send(own_quarter().at[:, features(j)], wout.at[back, core, r], (ctx, j), w_first).start()

    send_wout()

    drain(kv_in.at[pl.ds(1, PEERS - 1)], recv_sem.at[kv_first])
    summed = kv_part[pl.ds(pl.multiple_of(exp * share, share), share)].astype(jnp.float32)
    for i in range(1, PEERS):
        summed += kv_in[i].astype(jnp.float32)
    kv[m, r, core, x] = summed.astype(jnp.bfloat16)
    stride_moves = [
        send(kv.at[m, r, core, x], kv.at[m, r, core, x], deep(dz)) for dz in (2 * RING, RING, 3 * RING)
    ]
    for move in stride_moves:
        move.start()
    m4, m8, m12 = (m + 1) % RING, (m + 2) % RING, (m + 3) % RING

    def got(piece, move_number):
        return send(piece, piece, sibling, move_number)

    first_of_stride = used[-3]
    stride_in = [
        got(kv.at[mm, r, core, x], first_of_stride + n) for n, mm in enumerate((m8, m12, m4))
    ]

    r1, r2, r3 = (r + 1) % RING, (r + 2) % RING, (r + 3) % RING

    def far_part(rr, begin, rows):
        return qw.at[2, core, pl.ds(pl.multiple_of(rr * f + begin, f // 2), rows)]

    far_moves = [
        send(far_part(r, 0, f // 2), far_part(r, 0, f // 2), deep(2)),
        send(far_part(r, f // 2, f // 2), far_part(r, f // 2, f // 2), deep(depth - 2)),
        send(far_part(r, 0, f), far_part(r, 0, f), deep(1)),
        send(far_part(r, 0, f), far_part(r, 0, f), deep(depth - 1)),
    ]
    first_of_far = used[-4]
    far_in = [
        got(far_part(r2, 0, f // 2), first_of_far),
        got(far_part(r2, f // 2, f // 2), first_of_far + 1),
        got(far_part(r3, 0, f), first_of_far + 2),
        got(far_part(r1, 0, f), first_of_far + 3),
    ]
    qw_moves[2].wait_recv()
    for move in far_moves:
        move.start()

    tok_moves[3].wait_recv()
    tok_moves["2a"].start()
    tok_moves[1].wait_recv()
    tok_moves["2b"].start()

    low_m, high_m = pl.ds(0, RING // 2), pl.ds(RING // 2, RING // 2)
    residue_moves = [
        send(kv.at[low_m, r, core, x], kv.at[low_m, r, core, x], deep(2)),
        send(kv.at[high_m, r, core, x], kv.at[high_m, r, core, x], deep(depth - 2)),
        send(kv.at[:, r, core, x], kv.at[:, r, core, x], deep(1)),
        send(kv.at[:, r, core, x], kv.at[:, r, core, x], deep(depth - 1)),
    ]
    first_of_residue = used[-4]
    residue_in = [
        got(kv.at[low_m, r2, core, x], first_of_residue),
        got(kv.at[high_m, r2, core, x], first_of_residue + 1),
        got(kv.at[:, r3, core, x], first_of_residue + 2),
        got(kv.at[:, r1, core, x], first_of_residue + 3),
    ]
    x1, x2, x3 = (x + 1) % RING, (x + 2) % RING, (x + 3) % RING
    x_numbers = {step: number_of() for step in (1, 3, 2)}
    x_moves = []

    def push_along_x(rr):
        for step in (1, 3, 2):
            piece = kv.at[:, rr, core, x]
            x_moves.append(send(piece, piece, place(0, step), x_numbers[step]))
            x_moves[-1].start()

    columns = (x, x3, x1, x2)
    across = [send(kv.at[:, :, core, xx], kv.at[:, :, core, xx], sibling) for xx in columns]
    first_across = used[-4]
    across_in = [got(kv.at[:, :, other_core, xx], first_across + n) for n, xx in enumerate(columns)]

    position = lax.broadcasted_iota(jnp.int32, (t, 128), 0)
    high = (position // 16).astype(jnp.float32).astype(jnp.bfloat16)
    low = (position % 16).astype(jnp.float32).astype(jnp.bfloat16)
    place_of = jnp.concatenate([high, low], axis=1)
    slots = lax.broadcasted_iota(jnp.int32, (capacity, t), 0).astype(jnp.float32)
    for n in range(RING * mine):
        line = (n // mine) * (RING * mine) + n % mine
        pick[n] = jnp.where(slot_row[line : line + 1, :] == slots, 1.0, 0.0).astype(jnp.bfloat16)
        found = dot(pick[n], place_of)
        where_row[n] = 16.0 * found[:, :128] + found[:, 128:]

    for move in stride_in:
        move.wait_recv()
    for move in residue_moves:
        move.start()
    push_along_x(r)

    pieces = PlaneGather.order()

    def fill_spread(begin, end):
        lanes = lax.broadcasted_iota(jnp.int32, (t, LANES), 1).astype(jnp.float32)
        for p in range(begin, end):
            part, slot = pieces[p]
            n = slot * mine + part
            spread[:, p * LANES : (p + 1) * LANES] = jnp.where(
                slot_of[:, n : n + 1] == lanes, gate_of[:, n : n + 1], 0.0
            ).astype(jnp.bfloat16)

    fill_spread(0, 8)
    residue_in[2].wait_recv()
    push_along_x(r3)
    residue_in[3].wait_recv()
    push_along_x(r1)
    residue_in[0].wait_recv()
    residue_in[1].wait_recv()
    push_along_x(r2)
    across[0].start()
    fill_spread(8, 12)
    load_wout.wait()
    drain(wout.at[pl.ds(1, PEERS - 1), core, r], recv_sem.at[w_first])
    low_s, high_s = pl.ds(0, PEERS // 2), pl.ds(PEERS // 2, PEERS // 2)
    w_moves = [
        send(wout.at[low_s, core, r], wout.at[low_s, core, r], deep(2)),
        send(wout.at[high_s, core, r], wout.at[high_s, core, r], deep(depth - 2)),
        send(wout.at[:, core, r], wout.at[:, core, r], deep(1)),
        send(wout.at[:, core, r], wout.at[:, core, r], deep(depth - 1)),
    ]
    first_of_w = used[-4]
    w_in = [
        got(wout.at[low_s, core, r2], first_of_w),
        got(wout.at[high_s, core, r2], first_of_w + 1),
        got(wout.at[:, core, r3], first_of_w + 2),
        got(wout.at[:, core, r1], first_of_w + 3),
    ]
    for move in w_moves:
        move.start()

    fill_spread(12, 16)


    qw_across, qw_across_in = {}, {}
    for dy in (1, 3, 2):
        slot = RING - dy
        for move in far_in if dy == 2 else [qw_moves[dy]]:
            move.wait_recv()
        qw_across[slot] = send(qw.at[slot, core], qw.at[slot, core], sibling)
        qw_across_in[slot] = got(qw.at[slot, other_core], used[-1])
        qw_across[slot].start()

    tok_moves["2a"].wait_recv()
    tok_moves["2b"].wait_recv()

    def partial_queries(dy):
        for part in range(2):
            rows = pl.ds(part * half, half)
            acc = jnp.zeros((half, mine * hd), jnp.float32)
            for dx in range(RING):
                own = features((x + dx) % RING)
                weight = jnp.concatenate([qw[dy, a, own] for a in range(mine)], axis=1)
                acc += dot(tok[dx, rows], weight)
            q_dense[rows] = acc.astype(jnp.bfloat16)
        for a in range(mine):
            q_part[dy, pl.ds(a * capacity, capacity)] = dot(
                pick[dy * mine + a], q_dense[:, a * hd : (a + 1) * hd]
            ).astype(jnp.bfloat16)

    q_part_moves = {
        dy: send(q_part.at[dy], q_part.at[2 * RING - dy], place(dy, 0)) for dy in range(1, RING)
    }
    for dy in (3, 1, 2):
        qw_across_in[dy].wait_recv()
        partial_queries(dy)
        q_part_moves[dy].start()
    load_qw.wait()
    partial_queries(0)

    fill_spread(16, 2 * PEERS)
    for dy in (3, 1, 2):
        q_part_moves[dy].wait_recv()
    q_all[0] = functools.reduce(
        jnp.add, [q_part[s].astype(jnp.float32) for s in (0, 5, 6, 7)]
    ).astype(jnp.bfloat16)
    q_moves = {dy: send(q_all.at[0], q_all.at[RING - dy], place(dy, 0)) for dy in range(1, RING)}
    for dy in (2, 1, 3):
        q_moves[dy].start()

    for n, step in enumerate((1, 3, 2)):
        drain(kv.at[:, :, core, columns[n + 1]], recv_sem.at[x_numbers[step]])
        across[n + 1].start()
    for move in across_in:
        move.wait_recv()

    factor = math.log2(math.e) / math.sqrt(hd)
    groups = z // 4
    span = RING * share
    block = 8 * span

    def attend(dy):
        top_score[...] = jnp.full_like(top_score, LOWEST)
        num[...] = jnp.zeros_like(num)

        def step(g, masked):
            keys = kv[g].reshape(block, 2 * hd)
            values = jnp.concatenate([keys[:, hd:], jnp.ones((block, hd), jnp.bfloat16)], axis=1)
            keys = keys[:, :hd]
            for a in range(mine):
                rows = pl.ds(a * capacity, capacity)
                scores = nt_dot(q_all[dy, rows], keys)
                if masked:
                    index = lax.broadcasted_iota(jnp.int32, (1, block), 1)
                    at = (8 * g + index // span - ctx) * t + y * span + index % span
                    scores = jnp.where(
                        at.astype(jnp.float32) <= where_row[dy * mine + a][:, 0:1], scores, LOWEST
                    )
                before = top_score[rows, 0:1]
                now = jnp.maximum(before, jnp.max(scores, axis=1, keepdims=True))
                weights = jnp.exp2((scores - now) * factor).astype(jnp.bfloat16)
                num[rows] = num[rows] * jnp.exp2((before - now) * factor) + dot(weights, values)
                top_score[rows] = jnp.broadcast_to(now, (capacity, 128))

        @pl.loop(0, groups)
        def _(g):
            step(g, False)

        step(groups, True)
        for a in range(mine):
            rows = pl.ds(a * capacity, capacity)
            norm = num[rows, hd:]
            part_out[dy, rows] = (num[rows, :hd] / norm).astype(jnp.bfloat16)
            lse = top_score[rows, 0:1] * factor + jnp.log2(norm[:, 0:1])
            part_lse[dy, pl.ds(a * 8, 8)] = to_row(lse)

    def diagonal():
        return lax.broadcasted_iota(jnp.int32, (capacity, LANES), 0) == lax.broadcasted_iota(
            jnp.int32, (capacity, LANES), 1
        )

    def to_row(values):
        row = jnp.sum(jnp.where(diagonal(), values, 0.0), axis=0, keepdims=True)
        return jnp.broadcast_to(row, (8, LANES))

    def to_column(row):
        return jnp.sum(jnp.where(diagonal(), row, 0.0), axis=1, keepdims=True)

    moves = []
    for dy in (0, 1, 2, 3):
        if dy:
            q_moves[RING - dy].wait_recv()
        attend(dy)
        if dy:
            moves.append(send(part_out.at[dy], part_out.at[2 * RING - dy], place(dy, 0)))
            moves.append(send(part_lse.at[dy], part_lse.at[2 * RING - dy], place(dy, 0)))
            moves[-2].start()
            moves[-1].start()
        if dy == 0:
            for move in w_in:
                move.wait_recv()
            w_across = send(wout.at[:, core], wout.at[:, core], sibling)
            w_across_in = got(wout.at[:, other_core], used[-1])
            w_across.start()

    produced[...] = jnp.zeros_like(produced)
    for move in moves:
        move.wait_recv()
    for a in range(mine):
        rows = pl.ds(a * capacity, capacity)
        parts = (0, 5, 6, 7)
        lses = [to_column(part_lse[s, pl.ds(a * 8, 1)]) for s in parts]
        top = functools.reduce(jnp.maximum, lses)
        weights = [jnp.exp2(lse - top) for lse in lses]
        norm = functools.reduce(jnp.add, weights)
        rows_sum = functools.reduce(
            jnp.add, [w * part_out[s, rows].astype(jnp.float32) for w, s in zip(weights, parts)]
        )
        heads[0, rows] = (rows_sum / norm).astype(jnp.bfloat16)

    seen = []

    def make_output(part, slot):
        begin = len(seen) * LANES
        seen.append((part, slot))
        made = dot(heads[slot, pl.ds(part * capacity, capacity)], wout[slot, part].reshape(hd, f))
        produced[begin : begin + capacity] = made.astype(jnp.bfloat16)

    added = [0]

    def beside(stage):
        if stage == 0:
            w_across_in.wait_recv()
        else:
            begin, end = added[0] * LANES, len(seen) * LANES
            part = dot(spread[:, begin:end], produced[begin:end])
            if stage == 1:
                total[...] = part
            elif stage < 4:
                total[...] += part
            else:
                out[...] = (total[...] + part).astype(jnp.bfloat16)
            added[0] = len(seen)

    head_gather = PlaneGather(heads, mine * capacity, head_send, head_recv, place)
    head_gather.run(make_output, beside)
    assert seen == pieces

    for step in (1, 3, 2):
        drain(kv.at[:, :, core, x], send_sem.at[x_numbers[step]])
    head_gather.finish()
    drain(kv_in.at[pl.ds(1, PEERS - 1)], send_sem.at[kv_first])
    drain(wout.at[pl.ds(1, PEERS - 1), core, r], send_sem.at[w_first])
    for copy in (
        *qw_moves.values(),
        *far_moves,
        *tok_moves.values(),
        *stride_moves,
        *residue_moves,
        *across,
        *w_moves,
        *qw_across.values(),
        *q_part_moves.values(),
        *q_moves.values(),
        *moves,
        w_across,
    ):
        copy.wait_send()


def per_device(depth, tokens, expert_ids, gates, query_weight, key_weight, value_weight, output_weight):
    t, f = tokens.shape
    routes = expert_ids.shape[1]
    mine, model, hd = query_weight.shape
    experts = mine * PEERS
    capacity = min(t, max(2, 5 * t * routes // (4 * experts)))
    owned = mine * capacity
    share = t // PEERS
    bf16, f32 = jnp.bfloat16, jnp.float32
    vmem, anywhere = pl.BlockSpec(memory_space=pltpu.VMEM), pl.BlockSpec(memory_space=pl.ANY)
    return pl.pallas_call(
        functools.partial(layer, capacity, depth),
        out_shape=jax.ShapeDtypeStruct((t, f), bf16),
        in_specs=[vmem, vmem, vmem, anywhere, vmem, vmem, anywhere],
        out_specs=vmem,
        scratch_shapes=[
            pltpu.VMEM((RING, t, f), bf16),
            pltpu.VMEM((RING, mine, RING * f, hd), bf16),
            pltpu.VMEM((t, 2 * hd), bf16),
            pltpu.VMEM((PEERS, share, 2 * hd), bf16),
            pltpu.VMEM((depth // RING, RING, 2, RING, share, 2 * hd), bf16),
            pltpu.VMEM((t, mine * hd), bf16),
            pltpu.VMEM((2 * RING, owned, hd), bf16),
            pltpu.VMEM((RING, owned, hd), bf16),
            pltpu.VMEM((t, 128), f32),
            pltpu.VMEM((t, 128), f32),
            pltpu.VMEM((128, t), f32),
            pltpu.VMEM((t, experts * LANES), bf16),
            pltpu.VMEM((RING * mine, capacity, t), bf16),
            pltpu.VMEM((RING * mine, capacity, 128), f32),
            pltpu.VMEM((PEERS, mine, RING, hd // RING, f), bf16),
            pltpu.VMEM((owned, 128), f32),
            pltpu.VMEM((owned, 2 * hd), f32),
            pltpu.VMEM((2 * RING, owned, hd), bf16),
            pltpu.VMEM((2 * RING, 8 * mine, LANES), f32),
            pltpu.VMEM((PEERS, owned, hd), bf16),
            pltpu.VMEM((experts * LANES, f), bf16),
            pltpu.VMEM((t, f), f32),
            pltpu.SemaphoreType.DMA((40,)),
            pltpu.SemaphoreType.DMA((40,)),
            pltpu.SemaphoreType.DMA((64,)),
            pltpu.SemaphoreType.DMA((64,)),
            pltpu.SemaphoreType.DMA((2,)),
        ],
        compiler_params=pltpu.CompilerParams(
            collective_id=0, has_side_effects=True, vmem_limit_bytes=56 * 1024 * 1024
        ),
    )(tokens, expert_ids.T, gates.T, query_weight, key_weight, value_weight, output_weight)


def solution(mesh):
    in_specs = (
        P("ctx", "exp"),
        P("ctx", None),
        P("ctx", None),
        P("exp", None, None),
        P("exp", None),
        P("exp", None),
        P("exp", None, None),
    )
    out_specs = P("ctx", "exp")
    return jax.shard_map(
        functools.partial(per_device, mesh.shape["ctx"] // 2),
        mesh=mesh,
        in_specs=in_specs,
        out_specs=out_specs,
        check_vma=False,
    )
```
